128 devices in a mesh: dp: 8 (over x_lo, z), expert: 16 (over y, x_hi, core).
Axes of the slice: x: 4 (x_hi: 2, x_lo: 2; x = x_hi * 2 + x_lo), y: 4, z: 4, core: 2. Of those that a mesh axis runs over, the one named last changes fastest.
Arguments:
- tokens: bfloat16 [2048, 128, 1280], P(('dp', 'expert')), may hold values from -16 to 16
- slot_params: bfloat16 [1280, 16], replicated, may hold values from -1 to 1
- grad_out: bfloat16 [2048, 128, 1280], P(('dp', 'expert')), may hold values from -6 to 6
- slot_codes: int32 [2048, 16, 1280], P('dp', 'expert'), may hold values from 0 to 254, as said below
- scale_exps: int32 [2048, 16, 10], P('dp', 'expert'), may hold values from -9 to -7
- w_in: bfloat16 [16, 1280, 5120], P('expert', None, 'dp'), may hold values from -0.15625 to 0.15625
- w_out: bfloat16 [16, 5120, 1280], P('expert', 'dp'), may hold values from -0.078125 to 0.078125
Outputs:
- grad_tokens: bfloat16 [2048, 128, 1280], P(('dp', 'expert'))
- grad_params: float32 [1280, 16], replicated
- grad_w_in: bfloat16 [16, 1280, 5120], P('expert', None, 'dp')
- grad_w_out: bfloat16 [16, 5120, 1280], P('expert', 'dp')
The draws below stay inside these ranges and needn't reach their ends.
Inputs may be any that keep to these rules, and one draw needn't show every extreme that they name: `slot_codes`: codes 127 and 255 never occur.
All inputs are finite; a program needn't handle non-finite values.
Results may differ from the reference program's by a relative error of at most 0.015.
Values may be sent and summed in bfloat16 or wider, within the bound.
A program may use at most 192 MiB of HBM per device.

```python
import math
import jax
import jax.numpy as jnp

D = 1280
FF = 5120
PATCHES = 128
QBLOCK = 128
EXPERTS = 16
IMAGES = 2048


def router_parts(key):
    normal_part = jax.random.normal(key, (D, EXPERTS), jnp.float32)
    return normal_part


def draw_slot_params(key, part):
    normal_part = router_parts(key)
    return jnp.clip(normal_part * (3.0 / math.sqrt(D)), -1.0, 1.0).astype(jnp.bfloat16)


def draw_tokens(key, part):
    key = jax.random.fold_in(key, 23)
    key_vals = jax.random.fold_in(key, 0)
    return jnp.clip(jax.random.normal(key_vals, (IMAGES, PATCHES, D), jnp.float32), -6.0, 6.0).astype(jnp.bfloat16)


def draw_slot_codes(key, part):
    key = jax.random.fold_in(key, 5)
    raw_codes = jax.random.randint(key, (IMAGES, EXPERTS, D), 0, 254)
    return raw_codes + (raw_codes >= 127).astype(jnp.int32)


def touch_ends(result, stream_key, low, largest):
    index_at = [jax.random.randint(jax.random.fold_in(stream_key, axis), (), 0, length) for axis, length in enumerate(result.shape)]
    widest = result.shape.index(max(result.shape))
    beside = index_at[:widest] + [(index_at[widest] + 1) % result.shape[widest]] + index_at[widest + 1:]
    return result.at[tuple(index_at)].set(low).at[tuple(beside)].set(largest)


def level_of(key, shape, cuts, low, top_value):
    def one(position, shards_of):
        steps = jax.random.uniform(jax.random.fold_in(jax.random.fold_in(key, 6), position), (shards_of,), jnp.float32, low / len(cuts), top_value / len(cuts))
        return jnp.repeat(jnp.exp(steps), shape[position] // shards_of).reshape((-1,) + (1,) * (len(shape) - position - 1))

    level = one(*cuts[0])
    for cut in cuts[1:]:
        level = level * one(*cut)
    return level


def scatter_about(stream_key, shape, width, reach, shards=(), kind=jnp.bfloat16):
    gain = level_of(stream_key, shape, shards, -0.22, 0.18) if shards else 1.0
    array = jax.random.normal(stream_key, shape, jnp.float32) * width * gain
    return jnp.minimum(jnp.maximum(array, -reach), reach).astype(kind)


def setup_inputs(seed: int = 0) -> dict:
    arg_keys = jax.random.split(jax.random.key(seed), 8)
    tokens = draw_tokens(jax.random.fold_in(arg_keys[7], 71), 0)
    slot_params = draw_slot_params(jax.random.fold_in(arg_keys[7], 71), 0)
    grad_out = scatter_about(arg_keys[2], (IMAGES, PATCHES, D), 1.0, 6.0, ((0, 128),))
    slot_codes = draw_slot_codes(jax.random.fold_in(arg_keys[7], 71), 0)
    scale_exps = touch_ends(jax.random.randint(arg_keys[4], (IMAGES, EXPERTS, D // QBLOCK), -9, -6), jax.random.fold_in(arg_keys[4], 1), -9, (-6) - 1).astype(jnp.int32)
    w_in = scatter_about(arg_keys[5], (EXPERTS, D, FF), D ** -0.5, 0.15625, ((0, 16), (2, 8)))
    w_out = scatter_about(arg_keys[6], (EXPERTS, FF, D), FF ** -0.5, 0.078125, ((0, 16), (1, 8)))
    return {"tokens": tokens, "slot_params": slot_params, "grad_out": grad_out, "slot_codes": slot_codes, "scale_exps": scale_exps, "w_in": w_in, "w_out": w_out}


gelu_coef = 0.7978845608028654


def gelu_both(pre_act):
    inner_arg = gelu_coef * (pre_act + 0.044715 * pre_act * pre_act * pre_act)
    tanh_val = jnp.tanh(inner_arg)
    active = 0.5 * pre_act * (1.0 + tanh_val)
    slope = 0.5 * (1.0 + tanh_val) + 0.5 * pre_act * (1.0 - tanh_val * tanh_val) * gelu_coef * (1.0 + 3.0 * 0.044715 * pre_act * pre_act)
    return active, slope


def decode_slots(slot_codes, exponents):
    sign_bit = slot_codes // 128
    exponent = (slot_codes // 8) % 16
    mantissa = (slot_codes % 8).astype(jnp.float32)
    normal_mag = (1.0 + mantissa / 8.0) * jnp.exp2((exponent - 7).astype(jnp.float32))
    small_mag = mantissa / 8.0 * (1.0 / 64.0)
    magnitude = jnp.where(exponent == 0, small_mag, normal_mag)
    decoded = (1.0 - 2.0 * sign_bit.astype(jnp.float32)) * magnitude
    full_shape = slot_codes.shape
    blocks = decoded.reshape(full_shape[:-1] + (full_shape[-1] // QBLOCK, QBLOCK))
    scaled = blocks * jnp.exp2(exponents.astype(jnp.float32))[..., None]
    return scaled.reshape(full_shape).astype(jnp.bfloat16)


def reference(tokens, slot_params, grad_out, slot_codes, scale_exps, w_in, w_out):
    tok32 = tokens.astype(jnp.float32)
    par32 = slot_params.astype(jnp.float32)
    logits = jnp.einsum("bmd,ds->bsm", tok32, par32)
    dispatch = jax.nn.softmax(logits, axis=2)
    combine = jax.nn.softmax(logits, axis=1)
    slot_in = decode_slots(slot_codes, scale_exps)
    pre_act = jnp.einsum("bsd,sdf->bsf", slot_in.astype(jnp.float32), w_in.astype(jnp.float32))
    active, slope = gelu_both(pre_act)
    hidden = active.astype(jnp.bfloat16)
    slot_out = jnp.einsum("bsf,sfd->bsd", hidden.astype(jnp.float32), w_out.astype(jnp.float32)).astype(jnp.bfloat16)
    comb_bf = combine.astype(jnp.bfloat16)
    slot_grad = jnp.einsum("bsm,bmd->bsd", comb_bf.astype(jnp.float32), grad_out.astype(jnp.float32)).astype(jnp.bfloat16)
    comb_grad = jnp.einsum("bmd,bsd->bsm", grad_out.astype(jnp.float32), slot_out.astype(jnp.float32))
    logit_comb = combine * (comb_grad - jnp.sum(combine * comb_grad, axis=1, keepdims=True))
    hidden_grad = jnp.einsum("bsd,sfd->bsf", slot_grad.astype(jnp.float32), w_out.astype(jnp.float32))
    pre_grad = (hidden_grad * slope).astype(jnp.bfloat16)
    grad_w_out = jnp.einsum("bsf,bsd->sfd", hidden.astype(jnp.float32), slot_grad.astype(jnp.float32)).astype(jnp.bfloat16)
    grad_w_in = jnp.einsum("bsd,bsf->sdf", slot_in.astype(jnp.float32), pre_grad.astype(jnp.float32)).astype(jnp.bfloat16)
    slot_in_grad = jnp.einsum("bsf,sdf->bsd", pre_grad.astype(jnp.float32), w_in.astype(jnp.float32)).astype(jnp.bfloat16)
    disp_grad = jnp.einsum("bmd,bsd->bsm", tok32, slot_in_grad.astype(jnp.float32))
    logit_disp = dispatch * (disp_grad - jnp.sum(dispatch * disp_grad, axis=2, keepdims=True))
    logit_grad = (logit_comb + logit_disp).astype(jnp.bfloat16)
    disp_bf = dispatch.astype(jnp.bfloat16)
    through_slots = jnp.einsum("bsm,bsd->bmd", disp_bf.astype(jnp.float32), slot_in_grad.astype(jnp.float32))
    through_logits = jnp.einsum("bsm,ds->bmd", logit_grad.astype(jnp.float32), par32)
    grad_tokens = (through_slots + through_logits).astype(jnp.bfloat16)
    grad_params = jnp.einsum("bmd,bsm->ds", tok32, logit_grad.astype(jnp.float32))
    return grad_tokens, grad_params, grad_w_in, grad_w_out
```

```python
import jax
import jax.numpy as jnp
from jax import lax
from jax.sharding import PartitionSpec as P

F32 = jnp.float32
BF16 = jnp.bfloat16
AXES = ("dp", "expert")
gelu_coef = 0.7978845608028654


def permutation(target):
    pairs = []
    for d in range(8):
        for e in range(16):
            x, z = target(d // 4, d % 4, e % 2)
            pairs.append((d * 16 + e, (x * 4 + z) * 16 + e))
    return pairs


def near(z):
    return z ^ 1


def far(z):
    return 3 - z


PERM_X = permutation(lambda x, z, core: (1 - x, z))
PERM_PAIR = permutation(lambda x, z, core: (x, far(z) if core else near(z)))
PERM_GROUP = permutation(lambda x, z, core: (x, near(z) if core else far(z)))


def over_x(value):
    return lax.ppermute(value, AXES, PERM_X)


def over_pair(value):
    return lax.ppermute(value, AXES, PERM_PAIR)


def over_group(value):
    return lax.ppermute(value, AXES, PERM_GROUP)


def gather_rows(block):
    half = block.shape[0] // 2
    from_x = over_x(block)
    from_g = over_group(block)
    diag_1 = over_group(from_x[:half])
    diag_2 = over_x(from_g[half:])
    return jnp.concatenate([block, from_x, from_g, diag_1, diag_2], axis=0)


def scatter_rows(partial):
    rows = partial.shape[0] // 4
    half = rows // 2
    mine, for_x, for_g, for_d = (partial[i * rows : (i + 1) * rows] for i in range(4))
    got_1 = over_x(jnp.concatenate([for_x[:half], for_d[:half]], axis=0).astype(BF16))
    got_2 = over_group(jnp.concatenate([for_g[half:], for_d[half:]], axis=0).astype(BF16))
    send_1 = (for_g[:half] + got_1[half:].astype(F32)).astype(BF16)
    send_2 = (for_x[half:] + got_2[half:].astype(F32)).astype(BF16)
    last_1 = over_group(send_1)
    last_2 = over_x(send_2)
    out_1 = mine[:half] + got_1[:half].astype(F32) + last_1.astype(F32)
    out_2 = mine[half:] + got_2[:half].astype(F32) + last_2.astype(F32)
    return jnp.concatenate([out_1, out_2], axis=0).astype(BF16)


def sum_over_all(value):
    d, s = value.shape
    parts = lax.all_to_all(value.reshape(128, d // 128, s), AXES, split_axis=0, concat_axis=0, tiled=True)
    mine = jnp.sum(parts, axis=0, keepdims=True)
    copies = jnp.broadcast_to(mine, (128, d // 128, s))
    return lax.all_to_all(copies, AXES, split_axis=0, concat_axis=0, tiled=True).reshape(d, s)


def gelu_both(pre_act):
    inner_arg = gelu_coef * (pre_act + 0.044715 * pre_act * pre_act * pre_act)
    tanh_val = jnp.tanh(inner_arg)
    active = 0.5 * pre_act * (1.0 + tanh_val)
    slope = 0.5 * (1.0 + tanh_val) + 0.5 * pre_act * (1.0 - tanh_val * tanh_val) * gelu_coef * (
        1.0 + 3.0 * 0.044715 * pre_act * pre_act
    )
    return (active, slope)


def decode_slots(slot_codes, exponents, block_len):
    sign_bit = slot_codes // 128
    exponent = slot_codes // 8 % 16
    mantissa = (slot_codes % 8).astype(F32)
    normal_mag = (1.0 + mantissa / 8.0) * jnp.exp2((exponent - 7).astype(F32))
    small_mag = mantissa / 8.0 * (1.0 / 64.0)
    magnitude = jnp.where(exponent == 0, small_mag, normal_mag)
    decoded = (1.0 - 2.0 * sign_bit.astype(F32)) * magnitude
    full_shape = slot_codes.shape
    blocks = decoded.reshape(full_shape[:-1] + (full_shape[-1] // block_len, block_len))
    scaled = blocks * jnp.exp2(exponents.astype(F32))[..., None]
    return scaled.reshape(full_shape).astype(BF16)


def dot(a, b, dims):
    return lax.dot_general(a, b, (dims, ((), ())), preferred_element_type=F32)


def local(tokens, slot_params, grad_out, slot_codes, scale_exps, w_in, w_out):
    w_in_own, w_out_own = w_in[0], w_out[0]
    w_in_par = over_pair(w_in_own)
    block_len = slot_codes.shape[2] // scale_exps.shape[2]
    slot_in = decode_slots(slot_codes[:, 0], scale_exps[:, 0], block_len)
    all_in = gather_rows(slot_in)

    logits = jnp.einsum("bmd,ds->bsm", tokens, slot_params, preferred_element_type=F32)
    combine = jax.nn.softmax(logits, axis=1)
    comb_bf = combine.astype(BF16)
    slot_grad = jnp.einsum("bsm,bmd->bsd", comb_bf, grad_out, preferred_element_type=F32).astype(BF16)
    recv_grad = lax.all_to_all(slot_grad, "expert", split_axis=1, concat_axis=0, tiled=True)
    w_out_par = over_pair(w_out_own)
    all_grad = gather_rows(recv_grad[:, 0])
    dispatch = jax.nn.softmax(logits, axis=2)

    act_own, slope_own = gelu_both(dot(all_in, w_in_own, ((1,), (0,))))
    act_par, slope_par = gelu_both(dot(all_in, w_in_par, ((1,), (0,))))
    hid_own, hid_par = act_own.astype(BF16), act_par.astype(BF16)
    part_out = dot(hid_own, w_out_own, ((1,), (0,))) + dot(hid_par, w_out_par, ((1,), (0,)))
    slot_out = scatter_rows(part_out)
    back_out = lax.all_to_all(slot_out[:, None], "expert", split_axis=0, concat_axis=1, tiled=True)

    pg_own = (dot(all_grad, w_out_own, ((1,), (1,))) * slope_own).astype(BF16)
    pg_par = (dot(all_grad, w_out_par, ((1,), (1,))) * slope_par).astype(BF16)
    part_grad = dot(pg_own, w_in_own, ((1,), (1,))) + dot(pg_par, w_in_par, ((1,), (1,)))
    slot_in_grad = scatter_rows(part_grad)
    back_grad = lax.all_to_all(slot_in_grad[:, None], "expert", split_axis=0, concat_axis=1, tiled=True)

    gw_out_got = over_pair(dot(hid_par, all_grad, ((0,), (0,))).astype(BF16))
    gw_in_got = over_pair(dot(all_in, pg_par, ((0,), (0,))).astype(BF16))
    grad_w_out = (dot(hid_own, all_grad, ((0,), (0,))) + gw_out_got.astype(F32)).astype(BF16)
    grad_w_in = (dot(all_in, pg_own, ((0,), (0,))) + gw_in_got.astype(F32)).astype(BF16)

    comb_grad = jnp.einsum("bmd,bsd->bsm", grad_out, back_out, preferred_element_type=F32)
    logit_comb = combine * (comb_grad - jnp.sum(combine * comb_grad, axis=1, keepdims=True))
    disp_grad = jnp.einsum("bmd,bsd->bsm", tokens, back_grad, preferred_element_type=F32)
    logit_disp = dispatch * (disp_grad - jnp.sum(dispatch * disp_grad, axis=2, keepdims=True))
    logit_grad = (logit_comb + logit_disp).astype(BF16)
    disp_bf = dispatch.astype(BF16)
    local_params = jnp.einsum("bmd,bsm->ds", tokens, logit_grad, preferred_element_type=F32)
    grad_params = sum_over_all(local_params)
    through_slots = jnp.einsum("bsm,bsd->bmd", disp_bf, back_grad, preferred_element_type=F32)
    through_logits = jnp.einsum("bsm,ds->bmd", logit_grad, slot_params, preferred_element_type=F32)
    grad_tokens = (through_slots + through_logits).astype(BF16)
    return (grad_tokens, grad_params, grad_w_in[None], grad_w_out[None])


def solution(mesh):
    in_specs = (
        P(("dp", "expert"), None, None),
        P(),
        P(("dp", "expert"), None, None),
        P("dp", "expert", None),
        P("dp", "expert", None),
        P("expert", None, "dp"),
        P("expert", "dp", None),
    )
    out_specs = (
        P(("dp", "expert"), None, None),
        P(),
        P("expert", None, "dp"),
        P("expert", "dp", None),
    )
    return jax.shard_map(local, mesh=mesh, in_specs=in_specs, out_specs=out_specs, check_vma=False)
```

```python
import jax
import jax.numpy as jnp
from jax import lax
from jax.experimental import pallas as pl
from jax.experimental.pallas import tpu as pltpu
from jax.sharding import PartitionSpec as P

F32 = jnp.float32
BF16 = jnp.bfloat16
MESH = pl.DeviceIdType.MESH
gelu_coef = 0.7978845608028654

D, FU = 1280, 640
IMG, PAT, S = 16, 128, 16
ROWS, UNIT = 1024, 128
ND, NE = 8, 16

X1, D1, G2, D2, M1, M2, G1, X2 = range(8)

W_IN, W_OUT = 0, 1
IN_HOP, GR_HOP, OUT_RS, IG_RS = 2, 8, 14, 18
GWO, GWI = 22, 27
A2A_G, A2A_O, A2A_I = 32, 33, 34
GP_A, GP_B, GP_C = 35, 36, 37
N_SEM = 38
L_CODE, L_WIN, L_WOUT, L_TOK, L_GO, L_GT, L_GWO, L_GWI, L_GP = 0, 1, 2, 3, 7, 11, 15, 20, 25
N_LOC = 26


def dot(a, b, ca, cb):
    return lax.dot_general(a, b, (((ca,), (cb,)), ((), ())), preferred_element_type=F32)


def gelu_both(x):
    x2 = x * x
    t = jnp.tanh(gelu_coef * (x + 0.044715 * x * x2))
    h = 0.5 * (1.0 + t)
    return x * h, h + 0.5 * x * (1.0 - t * t) * (gelu_coef + (gelu_coef * 3.0 * 0.044715) * x2)


def unit(u, n=1):
    return pl.ds(u * UNIT, n * UNIT)


def put(ref, rows, value):
    for j in range(D // 128):
        ref[j, rows, :] = value[:, j * 128 : (j + 1) * 128]


def every_16th(ref, start):
    return jnp.concatenate([ref[j, pl.ds(start, 16, stride=16), :].astype(BF16) for j in range(D // 128)], axis=1)


def kernel(
    codes, scales, tokens, gout, par_t, w_in, w_out,
    gt_out, gp_out, gwi_out, gwo_out,
    code_v, tok, go, win, wout, rin, rgr, hid, slope, pg,
    comb, disp, fbuf, gbuf, sg_send, back_o, back_i,
    ps_o, ps_i, kp_o, kp_i, rs_o, rs_i, h2_o, h2_i, fin_o, fin_i,
    gwo_s, gwi_s, gwo_r, gwi_r, gp_acc, gp_s, gp_r1, gp_m, gp_r2, gp_f,
    s_sem, r_sem, l_sem,
):
    d, e = lax.axis_index("dp"), lax.axis_index("expert")
    xl, z, core = d // 4, lax.rem(d, 4), lax.rem(e, 2)
    z_near = z + 1 - 2 * lax.rem(z, 2)
    z_far = 3 - z
    z_pair = z_near * (1 - core) + z_far * core
    z_group = z_far * (1 - core) + z_near * core
    dev_x = ((1 - xl) * 4 + z, e)
    dev_p = (xl * 4 + z_pair, e)
    dev_g = (xl * 4 + z_group, e)
    others_e = [(d, lax.rem(e + k, NE)) for k in range(1, NE)]
    others_d = [(lax.rem(d + k, ND), e) for k in range(1, ND)]

    def remote(src, dst, i, dev):
        return pltpu.make_async_remote_copy(
            src_ref=src, dst_ref=dst, send_sem=s_sem.at[i], recv_sem=r_sem.at[i], device_id=dev, device_id_type=MESH
        )

    def here(src, dst, i):
        return pltpu.make_async_copy(src, dst, l_sem.at[i])

    cp_code = here(codes, code_v, L_CODE)
    cp_win = here(w_in.at[0], win.at[0], L_WIN)
    cp_wout = here(w_out.at[0], wout.at[0], L_WOUT)
    cp_code.start()

    def tok_copy(c):
        return here(tokens.at[pl.ds(c * 4, 4)], tok.at[pl.ds(c * 4, 4)], L_TOK + c)

    def go_copy(c):
        return here(gout.at[pl.ds(c * 4, 4)], go.at[pl.ds(c * 4, 4)], L_GO + c)

    for c in range(4):
        tok_copy(c).start()
        go_copy(c).start()
    cp_win.start()
    cp_wout.start()

    barrier = pltpu.get_barrier_semaphore()
    for dev in others_e + others_d:
        pl.semaphore_signal(barrier, inc=1, device_id=dev, device_id_type=MESH)
    pl.semaphore_wait(barrier, NE + ND - 2)

    c_win = remote(w_in.at[0], win.at[1], W_IN, dev_p)
    c_wout = remote(w_out.at[0], wout.at[1], W_OUT, dev_p)
    c_win.start()

    def row_hops(buf, base):
        first = [
            remote(buf.at[unit(M1)], buf.at[unit(X1)], base, dev_x),
            remote(buf.at[unit(M2)], buf.at[unit(G2)], base + 1, dev_g),
            remote(buf.at[unit(M2)], buf.at[unit(X2)], base + 2, dev_x),
            remote(buf.at[unit(M1)], buf.at[unit(G1)], base + 3, dev_g),
        ]
        second = [
            remote(buf.at[unit(X1)], buf.at[unit(D1)], base + 4, dev_g),
            remote(buf.at[unit(G2)], buf.at[unit(D2)], base + 5, dev_x),
        ]
        return first, second

    cp_code.wait()

    def decode(t, carry):
        r = pl.ds(pl.multiple_of(t * 32, 32), 32)
        to = pl.ds(pl.multiple_of(M1 * UNIT + t * 32, 32), 32)
        sc = scales[r, :]
        scale = jnp.where(sc == -9, 2.0**-18, jnp.where(sc == -8, 2.0**-17, 2.0**-16)).astype(F32)
        for j in range(D // 128):
            code = code_v[r, j * 128 : (j + 1) * 128]
            exp = (code >> 3) & 15
            man = code & 7
            mag = jnp.where(exp == 0, man, (man + 8) << jnp.maximum(exp - 1, 0))
            val = jnp.where(code >= 128, -mag, mag).astype(F32) * scale[:, j : j + 1]
            rin[to, j * 128 : (j + 1) * 128] = val.astype(BF16)
        return carry

    lax.fori_loop(0, 8, decode, 0)
    in_1, in_2 = row_hops(rin, IN_HOP)
    for c in in_1:
        c.start()

    def head(c, carry):
        tok_copy(c).wait()
        go_copy(c).wait()
        for k in range(4):
            i = c * 4 + k
            logits = dot(par_t[...], tok[i], 1, 1)
            e_m = jnp.exp(logits - jnp.max(logits, axis=1, keepdims=True))
            disp[i] = e_m / jnp.sum(e_m, axis=1, keepdims=True)
            e_s = jnp.exp(logits - jnp.max(logits, axis=0, keepdims=True))
            comb_i = e_s / jnp.sum(e_s, axis=0, keepdims=True)
            comb[i] = comb_i
            put(fbuf, pl.ds(pl.multiple_of(i * S, S), S), dot(comb_i.astype(BF16), go[i], 1, 0))
        return carry

    lax.fori_loop(0, 4, head, 0)
    for s in range(S):
        sg_send[s] = every_16th(fbuf, s)
    mine_16 = pl.ds(pl.multiple_of(e * IMG, IMG), IMG)
    at_me = pl.ds(pl.multiple_of(M1 * UNIT + e * IMG, IMG), IMG)
    for dev in others_e:
        remote(sg_send.at[dev[1]], rgr.at[at_me], A2A_G, dev).start()
    rgr[at_me, :] = sg_send[e]

    def wait_15(buf, i):
        both = remote(buf.at[pl.ds(0, 15 * IMG)], buf.at[pl.ds(0, 15 * IMG)], i, dev_x)
        both.wait()

    for c in in_1:
        c.wait_recv()
    for c in in_2:
        c.start()

    def pre(k, lo):
        a, sl = gelu_both(dot(rin[pl.ds(lo, 512), :], win[k], 1, 0))
        hid[k, pl.ds(lo, 512), :] = a.astype(BF16)
        slope[k, pl.ds(lo, 512), :] = sl.astype(BF16)

    cp_win.wait()
    cp_wout.wait()
    pre(0, 512)
    wait_15(rgr, A2A_G)
    gr_1, gr_2 = row_hops(rgr, GR_HOP)
    for c in gr_1:
        c.start()
    for c in in_2:
        c.wait_recv()
    pre(0, 0)
    c_win.wait()
    c_wout.start()
    pre(1, 512)
    for c in gr_1:
        c.wait_recv()
    for c in gr_2:
        c.start()
    pre(1, 0)

    def pre_grad(k, lo):
        hg = dot(rgr[pl.ds(lo, 512), :], wout[k], 1, 1)
        pg[k, pl.ds(lo, 512), :] = (hg * slope[k, pl.ds(lo, 512), :].astype(F32)).astype(BF16)

    pre_grad(0, 512)
    for c in gr_2:
        c.wait_recv()
    pre_grad(0, 0)

    def gwo_dot(k, c):
        return dot(hid[k, :, pl.ds(pl.multiple_of(c * 128, 128), 128)], rgr[...], 0, 0)

    def gwi_dot(k, c):
        return dot(rin[:, pl.ds(pl.multiple_of(c * 256, 256), 256)], pg[k], 0, 0)

    def gwo_copy(c):
        return remote(gwo_s.at[c], gwo_r.at[c], GWO + c, dev_p)

    def gwi_copy(c):
        return remote(gwi_s.at[c], gwi_r.at[c], GWI + c, dev_p)

    def send_gwo(c, carry):
        gwo_s[c] = gwo_dot(1, c).astype(BF16)
        gwo_copy(c).start()
        return carry

    lax.fori_loop(0, 5, send_gwo, 0)

    def part(act, w, cw, r):
        return dot(act[0, r, :], w[0], 1, cw) + dot(act[1, r, :], w[1], 1, cw)

    def rs_hops(ps, rs, h2, base):
        first = [
            remote(ps.at[unit(0, 2)], rs.at[unit(0, 2)], base, dev_x),
            remote(ps.at[unit(2, 2)], rs.at[unit(2, 2)], base + 1, dev_g),
        ]
        second = [
            remote(h2.at[unit(0)], rs.at[unit(4)], base + 2, dev_g),
            remote(h2.at[unit(1)], rs.at[unit(5)], base + 3, dev_x),
        ]
        return first, second

    c_wout.wait()
    out_1, out_2 = rs_hops(ps_o, rs_o, h2_o, OUT_RS)
    ig_1, ig_2 = rs_hops(ps_i, rs_i, h2_i, IG_RS)
    for t in range(2):
        ps_o[unit(2 * t, 2), :] = part(hid, wout, 0, unit(2 * t, 2)).astype(BF16)
        out_1[t].start()
    pre_grad(1, 0)
    for t in range(2):
        ps_i[unit(2 * t, 2), :] = part(pg, win, 1, unit(2 * t, 2)).astype(BF16)
        ig_1[t].start()
    for t in range(2):
        kp_o[unit(2 * t, 2), :] = part(hid, wout, 0, unit(4 + 2 * t, 2))
    pre_grad(1, 512)
    for t in range(2):
        kp_i[unit(2 * t, 2), :] = part(pg, win, 1, unit(4 + 2 * t, 2))

    def second_hop(first, second, kp, rs, h2):
        first[0].wait_recv()
        h2[unit(0), :] = (kp[unit(2), :] + rs[unit(1), :].astype(F32)).astype(BF16)
        second[0].start()
        first[1].wait_recv()
        h2[unit(1), :] = (kp[unit(3), :] + rs[unit(3), :].astype(F32)).astype(BF16)
        second[1].start()

    def finish_rows(second, kp, rs, fin, back, i):
        second[0].wait_recv()
        fin[unit(0), :] = (
            kp[unit(0), :] + rs[unit(0), :].astype(F32) + rs[unit(4), :].astype(F32)
        ).astype(BF16)
        second[1].wait_recv()
        fin[unit(1), :] = (
            kp[unit(1), :] + rs[unit(2), :].astype(F32) + rs[unit(5), :].astype(F32)
        ).astype(BF16)
        for dev in others_e:
            src = pl.ds(pl.multiple_of(dev[1] * IMG, IMG), IMG)
            remote(fin.at[src], back.at[mine_16], i, dev).start()
        back[mine_16, :] = fin[mine_16, :]

    second_hop(out_1, out_2, kp_o, rs_o, h2_o)

    def send_gwi(c, carry):
        gwi_s[c] = gwi_dot(1, c).astype(BF16)
        gwi_copy(c).start()
        return carry

    lax.fori_loop(0, 5, send_gwi, 0)
    second_hop(ig_1, ig_2, kp_i, rs_i, h2_i)
    finish_rows(out_2, kp_o, rs_o, fin_o, back_o, A2A_O)
    finish_rows(ig_2, kp_i, rs_i, fin_i, back_i, A2A_I)

    wait_15(back_o, A2A_O)
    put(fbuf, slice(None), back_o[...].astype(F32))

    def tail_comb(c, carry):
        for k in range(4):
            i = c * 4 + k
            cg = dot(every_16th(fbuf, i), go[i], 1, 1)
            cm = comb[i]
            comb[i] = cm * (cg - jnp.sum(cm * cg, axis=0, keepdims=True))
        return carry

    lax.fori_loop(0, 4, tail_comb, 0)
    wait_15(back_i, A2A_I)
    put(gbuf, slice(None), back_i[...].astype(F32))
    gp_acc[...] = jnp.zeros_like(gp_acc)

    def gt_copy(c):
        return here(tok.at[pl.ds(c * 4, 4)], gt_out.at[pl.ds(c * 4, 4)], L_GT + c)

    def tail(c, carry):
        for k in range(4):
            i = c * 4 + k
            bg = every_16th(gbuf, i)
            dg = dot(bg, tok[i], 1, 1)
            dp = disp[i]
            lg = (comb[i] + dp * (dg - jnp.sum(dp * dg, axis=1, keepdims=True))).astype(BF16)
            gp_acc[...] += dot(lg, tok[i], 1, 0)
            left = jnp.concatenate([dp.astype(BF16), lg], axis=0)
            right = jnp.concatenate([bg, par_t[...]], axis=0)
            tok[i] = dot(left, right, 0, 0).astype(BF16)
        gt_copy(c).start()
        return carry

    lax.fori_loop(0, 4, tail, 0)

    for s in range(S):
        gp_s[s] = gp_acc[s : s + 1, :]
    for dev in others_e:
        remote(gp_s.at[dev[1]], gp_r1.at[e], GP_A, dev).start()
    gp_r1[e] = gp_s[e]

    def finish_gwo(c, carry):
        own = gwo_dot(0, c)
        gwo_copy(c).wait()
        gwo_r[c] = (own + gwo_r[c].astype(F32)).astype(BF16)
        here(gwo_r.at[c], gwo_out.at[0, pl.ds(pl.multiple_of(c * 128, 128), 128)], L_GWO + c).start()
        return carry

    lax.fori_loop(0, 3, finish_gwo, 0)
    wait_many = remote(gp_s.at[pl.ds(0, NE - 1)], gp_r1.at[pl.ds(0, NE - 1)], GP_A, dev_x)
    wait_many.wait()
    total = gp_r1[0]
    for k in range(1, NE):
        total = total + gp_r1[k]
    gp_m[0] = total
    gp_r2[d] = total
    for dev in others_d:
        remote(gp_m.at[0], gp_r2.at[d], GP_B, dev).start()
    lax.fori_loop(3, 5, finish_gwo, 0)
    wait_many = remote(gp_r2.at[pl.ds(0, ND - 1)], gp_r2.at[pl.ds(0, ND - 1)], GP_B, dev_x)
    wait_many.wait()
    total = gp_r2[0]
    for k in range(1, ND):
        total = total + gp_r2[k]
    gp_m[1] = total
    gp_f[e] = total
    for dev in others_e:
        remote(gp_m.at[1], gp_f.at[e], GP_C, dev).start()

    def finish_gwi(c, carry):
        own = gwi_dot(0, c)
        gwi_copy(c).wait()
        gwi_r[c] = (own + gwi_r[c].astype(F32)).astype(BF16)
        here(gwi_r.at[c], gwi_out.at[0, pl.ds(pl.multiple_of(c * 256, 256), 256)], L_GWI + c).start()
        return carry

    lax.fori_loop(0, 5, finish_gwi, 0)
    wait_many = remote(gp_f.at[pl.ds(0, NE - 1)], gp_f.at[pl.ds(0, NE - 1)], GP_C, dev_x)
    wait_many.wait()
    cp_gp = here(gp_f, gp_out, L_GP)
    cp_gp.start()

    for c in in_1 + in_2 + gr_1 + gr_2 + out_1 + out_2 + ig_1 + ig_2:
        c.wait_send()
    for c in range(4):
        gt_copy(c).wait()
    for c in range(5):
        here(gwo_r.at[c], gwo_out.at[0, pl.ds(c * 128, 128)], L_GWO + c).wait()
        here(gwi_r.at[c], gwi_out.at[0, pl.ds(c * 256, 256)], L_GWI + c).wait()
    cp_gp.wait()


def layer(codes, scales, tokens, gout, par_t, w_in, w_out):
    any_space = pl.BlockSpec(memory_space=pl.ANY)
    vmem_space = pl.BlockSpec(memory_space=pltpu.VMEM)

    def buf(*shape, dtype=BF16):
        return pltpu.VMEM(shape, dtype)

    scratch = [
        buf(256, D, dtype=jnp.int32), buf(IMG, PAT, D), buf(IMG, PAT, D), buf(2, D, FU), buf(2, FU, D),
        buf(ROWS, D), buf(ROWS, D), buf(2, ROWS, FU), buf(2, ROWS, FU), buf(2, ROWS, FU),
        buf(IMG, S, PAT, dtype=F32), buf(IMG, S, PAT, dtype=F32), buf(D // 128, 256, 128, dtype=F32), buf(D // 128, 256, 128, dtype=F32),
        buf(S, IMG, D), buf(256, D), buf(256, D),
        buf(512, D), buf(512, D), buf(512, D, dtype=F32), buf(512, D, dtype=F32),
        buf(768, D), buf(768, D), buf(256, D), buf(256, D), buf(256, D), buf(256, D),
        buf(5, 128, D), buf(5, 256, FU), buf(5, 128, D), buf(5, 256, FU),
        buf(S, D, dtype=F32), buf(S, 1, D, dtype=F32), buf(S, 1, D, dtype=F32), buf(2, 1, D, dtype=F32),
        buf(ND, 1, D, dtype=F32), buf(S, 1, D, dtype=F32),
        pltpu.SemaphoreType.DMA((N_SEM,)), pltpu.SemaphoreType.DMA((N_SEM,)), pltpu.SemaphoreType.DMA((N_LOC,)),
    ]
    return pl.pallas_call(
        kernel,
        out_shape=(
            jax.ShapeDtypeStruct((IMG, PAT, D), BF16),
            jax.ShapeDtypeStruct((S, 1, D), F32),
            jax.ShapeDtypeStruct((1, D, FU), BF16),
            jax.ShapeDtypeStruct((1, FU, D), BF16),
        ),
        in_specs=[any_space, vmem_space, any_space, any_space, vmem_space, any_space, any_space],
        out_specs=(any_space,) * 4,
        scratch_shapes=scratch,
        compiler_params=pltpu.CompilerParams(
            collective_id=0, has_side_effects=True, vmem_limit_bytes=63 * 2**20
        ),
        cost_estimate=pl.CostEstimate(flops=21_000_000_000, bytes_accessed=40_000_000, transcendentals=2_000_000),
    )(codes, scales, tokens, gout, par_t, w_in, w_out)


def local(tokens, slot_params, grad_out, slot_codes, scale_exps, w_in, w_out):
    grad_tokens, grad_params, grad_w_in, grad_w_out = layer(
        slot_codes[:, 0], scale_exps[:, 0], tokens, grad_out, slot_params.T, w_in, w_out
    )
    return (grad_tokens, grad_params[:, 0].T, grad_w_in, grad_w_out)


def solution(mesh):
    in_specs = (
        P(("dp", "expert"), None, None),
        P(),
        P(("dp", "expert"), None, None),
        P("dp", "expert", None),
        P("dp", "expert", None),
        P("expert", None, "dp"),
        P("expert", "dp", None),
    )
    out_specs = (
        P(("dp", "expert"), None, None),
        P(),
        P("expert", None, "dp"),
        P("expert", "dp", None),
    )
    return jax.shard_map(local, mesh=mesh, in_specs=in_specs, out_specs=out_specs, check_vma=False)
```

```python
import jax
import jax.numpy as jnp
from jax import lax
from jax.experimental import pallas as pl
from jax.experimental.pallas import tpu as pltpu
from jax.sharding import PartitionSpec as P

F32 = jnp.float32
BF16 = jnp.bfloat16
MESH = pl.DeviceIdType.MESH
gelu_coef = 0.7978845608028654

D, FU = 1280, 640
IMG, PAT, S = 16, 128, 16
ROWS = 1024
ND, NE = 8, 16

N1, N2 = 64, 192
X1, D1, G2, D2 = (0, N1), (64, N1), (128, N2), (320, N2)
M1, M2, G1, X2 = (512, N1), (576, N2), (768, N1), (832, N2)
ME = 512
KEEP = 512

W_IN, W_OUT = 0, 1
IN_HOP, GR_HOP, OUT_RS, IG_RS = 2, 9, 16, 20
GWO, GWI = 24, 29
A2A_G, A2A_O, A2A_I = 34, 35, 36
GP_A, GP_B, GP_C = 37, 38, 39
N_SEM = 40
L_CODE, L_WIN, L_WOUT, L_TOK, L_GO, L_LEFT, L_BG, L_SC, L_GWO, L_GWI, L_GP = 0, 1, 2, 3, 7, 11, 12, 13, 15, 20, 25
N_LOC = 26


def dot(a, b, ca, cb):
    return lax.dot_general(a, b, (((ca,), (cb,)), ((), ())), preferred_element_type=F32)


def gelu_both(x):
    x2 = x * x
    t = jnp.tanh(gelu_coef * (x + 0.044715 * x * x2))
    h = 0.5 * (1.0 + t)
    return x * h, h + 0.5 * x * (1.0 - t * t) * (gelu_coef + (gelu_coef * 3.0 * 0.044715) * x2)


def unit(u, skip=0, n=None):
    return pl.ds(u[0] + skip, n or u[1] - skip)


def put(ref, rows, value):
    for j in range(D // 128):
        ref[j, rows, :] = value[:, j * 128 : (j + 1) * 128]


def every_16th(ref, start):
    return jnp.concatenate([ref[j, pl.ds(start, 16, stride=16), :].astype(BF16) for j in range(D // 128)], axis=1)


def kernel(
    codes, scales, tokens, gout, par_t, w_in, w_out,
    left_out, bg_out, gp_out, gwi_out, gwo_out,
    code_v, sc_v, tok, go, win, wout, rin, rgr, hid, slope, pg,
    comb, disp, fbuf, gbuf, sg_send, back_o, back_i,
    ps_o, ps_i, kp_o, kp_i, rs_o, rs_i, h2_o, h2_i, fin_o, fin_i,
    gwo_s, gwi_s, gwo_r, gwi_r, gp_acc, gp_s, gp_r1, gp_m, gp_r2, gp_f, left, bgi, lg_all, gwi_own,
    s_sem, r_sem, l_sem,
):
    d, e = lax.axis_index("dp"), lax.axis_index("expert")
    xl, z, core = d // 4, lax.rem(d, 4), lax.rem(e, 2)
    z_near = z + 1 - 2 * lax.rem(z, 2)
    z_far = 3 - z
    z_pair = z_near * (1 - core) + z_far * core
    z_group = z_far * (1 - core) + z_near * core
    dev_x = ((1 - xl) * 4 + z, e)
    dev_p = (xl * 4 + z_pair, e)
    dev_g = (xl * 4 + z_group, e)
    others_e = [(d, lax.rem(e + k, NE)) for k in range(1, NE)]
    others_d = [(lax.rem(d + k, ND), e) for k in range(1, ND)]

    def remote(src, dst, i, dev):
        return pltpu.make_async_remote_copy(
            src_ref=src, dst_ref=dst, send_sem=s_sem.at[i], recv_sem=r_sem.at[i], device_id=dev, device_id_type=MESH
        )

    def here(src, dst, i):
        return pltpu.make_async_copy(src, dst, l_sem.at[i])

    cp_code = here(codes.at[:, 0], code_v, L_CODE)
    cp_win = here(w_in.at[0], win.at[0], L_WIN)
    cp_wout = here(w_out.at[0], wout.at[0], L_WOUT)
    cp_sc = here(scales.at[:, 0], sc_v, L_SC)
    cp_code.start()
    cp_sc.start()

    def four(c):
        return pl.ds(pl.multiple_of(c * 4 * PAT, 4 * PAT), 4 * PAT)

    def image(i):
        return pl.ds(pl.multiple_of(i * PAT, PAT), PAT)

    def tok_copy(c):
        return here(tokens.at[four(c)], tok.at[four(c)], L_TOK + c)

    def go_copy(c):
        return here(gout.at[four(c)], go.at[four(c)], L_GO + c)

    barrier = pltpu.get_barrier_semaphore()
    for dev in others_e + others_d:
        pl.semaphore_signal(barrier, inc=1, device_id=dev, device_id_type=MESH)
    pl.semaphore_wait(barrier, NE + ND - 2)

    c_win = remote(w_in.at[0], win.at[1], W_IN, dev_p)
    c_wout = remote(w_out.at[0], wout.at[1], W_OUT, dev_p)
    c_win.start()

    def row_hops(buf, base):
        first = [
            remote(buf.at[unit(M1)], buf.at[unit(X1)], base, dev_x),
            remote(buf.at[unit(M2)], buf.at[unit(G2)], base + 1, dev_g),
            remote(buf.at[unit(M2)], buf.at[unit(X2)], base + 2, dev_x),
            remote(buf.at[unit(M1)], buf.at[unit(G1)], base + 3, dev_g),
        ]
        second = [
            remote(buf.at[unit(X1)], buf.at[unit(D1)], base + 4, dev_g),
            remote(buf.at[unit(X2, 0, 64)], buf.at[unit(D2, 0, 64)], base + 5, dev_g),
            remote(buf.at[unit(G2, 64)], buf.at[unit(D2, 64)], base + 6, dev_x),
        ]
        return first, second

    cp_code.wait()
    cp_sc.wait()

    sc = sc_v[...]
    fbuf[0, :, : D // 128] = jnp.where(sc == -9, 2.0**-18, jnp.where(sc == -8, 2.0**-17, 2.0**-16)).astype(F32).T

    def decode(t, carry):
        r = pl.ds(pl.multiple_of(t * 32, 32), 32)
        to = pl.ds(pl.multiple_of(ME + t * 32, 32), 32)
        scale = fbuf[0, r, : D // 128]
        for j in range(D // 128):
            code = code_v[r, j * 128 : (j + 1) * 128]
            exp = (code >> 3) & 15
            man = code & 7
            mag = jnp.where(exp == 0, man, (man + 8) << jnp.maximum(exp - 1, 0))
            val = jnp.where(code >= 128, -mag, mag).astype(F32) * scale[:, j : j + 1]
            rin[to, j * 128 : (j + 1) * 128] = val.astype(BF16)
        return carry

    lax.fori_loop(0, 8, decode, 0)
    in_1, in_2 = row_hops(rin, IN_HOP)
    for c in in_1:
        c.start()
    for c in range(4):
        tok_copy(c).start()
        go_copy(c).start()
    cp_win.start()
    cp_wout.start()

    def head(c, carry):
        tok_copy(c).wait()
        go_copy(c).wait()
        for k in range(4):
            i = c * 4 + k
            logits = dot(par_t[...], tok[image(i), :], 1, 1)
            e_m = jnp.exp(logits - jnp.max(logits, axis=1, keepdims=True))
            disp[i] = e_m / jnp.sum(e_m, axis=1, keepdims=True)
            e_s = jnp.exp(logits - jnp.max(logits, axis=0, keepdims=True))
            comb_i = e_s / jnp.sum(e_s, axis=0, keepdims=True)
            comb[i] = comb_i
            put(fbuf, pl.ds(pl.multiple_of(i * S, S), S), dot(comb_i.astype(BF16), go[image(i), :], 1, 0))
        return carry

    lax.fori_loop(0, 4, head, 0)
    for s in range(S):
        sg_send[s] = every_16th(fbuf, s)
    mine_16 = pl.ds(pl.multiple_of(e * IMG, IMG), IMG)
    at_me = pl.ds(pl.multiple_of(ME + e * IMG, IMG), IMG)
    for dev in others_e:
        remote(sg_send.at[dev[1]], rgr.at[at_me], A2A_G, dev).start()
    rgr[at_me, :] = sg_send[e]

    def wait_15(buf, i):
        both = remote(buf.at[pl.ds(0, 15 * IMG)], buf.at[pl.ds(0, 15 * IMG)], i, dev_x)
        both.wait()

    for c in in_1:
        c.wait_recv()
    for c in in_2:
        c.start()

    def pre(k, lo):
        a, sl = gelu_both(dot(rin[pl.ds(lo, 512), :], win[k], 1, 0))
        hid[k, pl.ds(lo, 512), :] = a.astype(BF16)
        slope[k, pl.ds(lo, 512), :] = sl.astype(BF16)

    cp_win.wait()
    cp_wout.wait()
    pre(0, 512)
    wait_15(rgr, A2A_G)
    gr_1, gr_2 = row_hops(rgr, GR_HOP)
    for c in gr_1:
        c.start()
    c_win.wait()
    c_wout.start()
    for c in in_2:
        c.wait_recv()
    pre(0, 0)
    pre(1, 512)
    for c in gr_1:
        c.wait_recv()
    for c in gr_2:
        c.start()
    pre(1, 0)

    def pre_grad(k, lo):
        hg = dot(rgr[pl.ds(lo, 512), :], wout[k], 1, 1)
        pg[k, pl.ds(lo, 512), :] = (hg * slope[k, pl.ds(lo, 512), :].astype(F32)).astype(BF16)

    pre_grad(0, 512)
    for c in gr_2:
        c.wait_recv()
    pre_grad(0, 0)

    def gwo_dot(k, c):
        return dot(hid[k, :, pl.ds(pl.multiple_of(c * 128, 128), 128)], rgr[...], 0, 0)

    def gwi_dot(k, c):
        return dot(rin[:, pl.ds(pl.multiple_of(c * 256, 256), 256)], pg[k], 0, 0)

    def gwo_copy(c):
        return remote(gwo_s.at[c], gwo_r.at[c], GWO + c, dev_p)

    def gwi_copy(c):
        return remote(gwi_s.at[c], gwi_r.at[c], GWI + c, dev_p)

    def fill_gwo(c, carry):
        gwo_s[c] = gwo_dot(1, c).astype(BF16)
        return carry

    lax.fori_loop(0, 5, fill_gwo, 0)

    def part(act, w, cw, r):
        return dot(act[0, r, :], w[0], 1, cw) + dot(act[1, r, :], w[1], 1, cw)

    def rs_hops(ps, rs, h2, base):
        first = [
            remote(ps.at[pl.ds(0, 2 * N1)], rs.at[pl.ds(0, 2 * N1)], base, dev_x),
            remote(ps.at[pl.ds(2 * N1, 2 * N2)], rs.at[pl.ds(2 * N1, 2 * N2)], base + 1, dev_g),
        ]
        second = [
            remote(h2.at[pl.ds(0, N1)], rs.at[pl.ds(512, N1)], base + 2, dev_g),
            remote(h2.at[pl.ds(N1, N2)], rs.at[pl.ds(512 + N1, N2)], base + 3, dev_x),
        ]
        return first, second

    def send_parts(act, w, cw, ps, first):
        for t in (1, 0):
            r = (pl.ds(0, 2 * N1), pl.ds(2 * N1, 2 * N2))[t]
            ps[r, :] = part(act, w, cw, r).astype(BF16)
            first[t].start()

    def keep_parts(act, w, cw, kp):
        for t in range(2):
            kp[pl.ds(t * 256, 256), :] = part(act, w, cw, pl.ds(KEEP + t * 256, 256))

    c_wout.wait()
    gwo_copy(0).start()
    out_1, out_2 = rs_hops(ps_o, rs_o, h2_o, OUT_RS)
    ig_1, ig_2 = rs_hops(ps_i, rs_i, h2_i, IG_RS)
    send_parts(hid, wout, 0, ps_o, out_1)
    pre_grad(1, 0)
    send_parts(pg, win, 1, ps_i, ig_1)
    keep_parts(hid, wout, 0, kp_o)
    pre_grad(1, 512)
    keep_parts(pg, win, 1, kp_i)

    def second_hop(first, second, kp, rs, h2):
        first[1].wait_recv()
        got = rs[pl.ds(2 * N1 + N2, N2), :].astype(F32)
        h2[pl.ds(N1, N2), :] = (kp[pl.ds(256 + N1, N2), :] + got).astype(BF16)
        second[1].start()
        first[0].wait_recv()
        got = rs[pl.ds(N1, N1), :].astype(F32)
        h2[pl.ds(0, N1), :] = (kp[pl.ds(256, N1), :] + got).astype(BF16)
        second[0].start()

    def finish_rows(second, kp, rs, fin, back, i):
        second[0].wait_recv()
        a, b, c = pl.ds(0, N1), pl.ds(0, N1), pl.ds(512, N1)
        fin[a, :] = (kp[a, :] + rs[b, :].astype(F32) + rs[c, :].astype(F32)).astype(BF16)
        second[1].wait_recv()
        a, b, c = pl.ds(N1, N2), pl.ds(2 * N1, N2), pl.ds(512 + N1, N2)
        fin[a, :] = (kp[a, :] + rs[b, :].astype(F32) + rs[c, :].astype(F32)).astype(BF16)
        for dev in others_e:
            src = pl.ds(pl.multiple_of(dev[1] * IMG, IMG), IMG)
            remote(fin.at[src], back.at[mine_16], i, dev).start()
        back[mine_16, :] = fin[mine_16, :]

    second_hop(out_1, out_2, kp_o, rs_o, h2_o)
    gwo_copy(1).start()

    def fill_gwi(c, carry):
        gwi_s[c] = gwi_dot(1, c).astype(BF16)
        return carry

    lax.fori_loop(0, 5, fill_gwi, 0)
    second_hop(ig_1, ig_2, kp_i, rs_i, h2_i)
    for c in range(2, 5):
        gwo_copy(c).start()
    for c in range(5):
        gwi_copy(c).start()
    finish_rows(out_2, kp_o, rs_o, fin_o, back_o, A2A_O)

    def fill_own(c, carry):
        gwi_own[c] = gwi_dot(0, c)
        return carry

    lax.fori_loop(0, 5, fill_own, 0)
    finish_rows(ig_2, kp_i, rs_i, fin_i, back_i, A2A_I)

    def finish_gwo(c, carry):
        own = gwo_dot(0, c)
        gwo_copy(c).wait()
        gwo_r[c] = (own + gwo_r[c].astype(F32)).astype(BF16)
        here(gwo_r.at[c], gwo_out.at[pl.ds(pl.multiple_of(c * 128, 128), 128)], L_GWO + c).start()
        return carry

    def finish_gwi(c, carry):
        gwi_copy(c).wait()
        gwi_r[c] = (gwi_own[c] + gwi_r[c].astype(F32)).astype(BF16)
        here(gwi_r.at[c], gwi_out.at[pl.ds(pl.multiple_of(c * 256, 256), 256)], L_GWI + c).start()
        return carry

    wait_15(back_o, A2A_O)
    put(fbuf, slice(None), back_o[...].astype(F32))

    def tail_comb(c, carry):
        for k in range(4):
            i = c * 4 + k
            cg = dot(every_16th(fbuf, i), go[image(i), :], 1, 1)
            cm = comb[i]
            comb[i] = cm * (cg - jnp.sum(cm * cg, axis=0, keepdims=True))
        return carry

    lax.fori_loop(0, 4, tail_comb, 0)
    wait_15(back_i, A2A_I)
    put(gbuf, slice(None), back_i[...].astype(F32))

    cp_left = here(left, left_out, L_LEFT)
    cp_bg = here(bgi, bg_out, L_BG)

    def tail(c, carry):
        for k in range(4):
            i = c * 4 + k
            bg = every_16th(gbuf, i)
            dg = dot(bg, tok[image(i), :], 1, 1)
            dp = disp[i]
            lg = (comb[i] + dp * (dg - jnp.sum(dp * dg, axis=1, keepdims=True))).astype(BF16)
            lg_all[:, image(i)] = lg
            left[i, :S] = dp.astype(BF16)
            left[i, S:] = lg
            bgi[i] = bg
        return carry

    lax.fori_loop(0, 4, tail, 0)
    cp_left.start()
    cp_bg.start()

    gp = dot(lg_all[...], tok[...], 1, 0)
    for s in range(S):
        gp_s[s] = gp[s : s + 1, :]
    for dev in others_e:
        remote(gp_s.at[dev[1]], gp_r1.at[e], GP_A, dev).start()
    gp_r1[e] = gp_s[e]

    lax.fori_loop(0, 5, finish_gwo, 0)
    wait_many = remote(gp_s.at[pl.ds(0, NE - 1)], gp_r1.at[pl.ds(0, NE - 1)], GP_A, dev_x)
    wait_many.wait()
    total = gp_r1[0]
    for k in range(1, NE):
        total = total + gp_r1[k]
    gp_m[0] = total
    gp_r2[d] = total
    for dev in others_d:
        remote(gp_m.at[0], gp_r2.at[d], GP_B, dev).start()
    lax.fori_loop(0, 2, finish_gwi, 0)
    wait_many = remote(gp_r2.at[pl.ds(0, ND - 1)], gp_r2.at[pl.ds(0, ND - 1)], GP_B, dev_x)
    wait_many.wait()
    total = gp_r2[0]
    for k in range(1, ND):
        total = total + gp_r2[k]
    gp_m[1] = total
    gp_f[e] = total
    for dev in others_e:
        remote(gp_m.at[1], gp_f.at[e], GP_C, dev).start()

    lax.fori_loop(2, 5, finish_gwi, 0)
    wait_many = remote(gp_f.at[pl.ds(0, NE - 1)], gp_f.at[pl.ds(0, NE - 1)], GP_C, dev_x)
    wait_many.wait()
    for s in range(S):
        gp_acc[s : s + 1, :] = gp_f[s]
    cp_gp = here(gp_acc, gp_out, L_GP)
    cp_gp.start()

    for c in in_1 + in_2 + gr_1 + gr_2 + out_1 + out_2 + ig_1 + ig_2:
        c.wait_send()
    cp_left.wait()
    cp_bg.wait()
    for c in range(5):
        here(gwo_r.at[c], gwo_out.at[pl.ds(c * 128, 128)], L_GWO + c).wait()
        here(gwi_r.at[c], gwi_out.at[pl.ds(c * 256, 256)], L_GWI + c).wait()
    cp_gp.wait()


def layer(codes, scales, tokens, gout, par_t, w_in, w_out):
    any_space = pl.BlockSpec(memory_space=pl.ANY)
    vmem_space = pl.BlockSpec(memory_space=pltpu.VMEM)

    def buf(*shape, dtype=BF16):
        return pltpu.VMEM(shape, dtype)

    scratch = [
        buf(256, D, dtype=jnp.int32), buf(D // 128, 256, dtype=jnp.int32), buf(IMG * PAT, D), buf(IMG * PAT, D), buf(2, D, FU), buf(2, FU, D),
        buf(ROWS, D), buf(ROWS, D), buf(2, ROWS, FU), buf(2, ROWS, FU), buf(2, ROWS, FU),
        buf(IMG, S, PAT, dtype=F32), buf(IMG, S, PAT, dtype=F32), buf(D // 128, 256, 128, dtype=F32), buf(D // 128, 256, 128, dtype=F32),
        buf(S, IMG, D), buf(256, D), buf(256, D),
        buf(512, D), buf(512, D), buf(512, D, dtype=F32), buf(512, D, dtype=F32),
        buf(768, D), buf(768, D), buf(256, D), buf(256, D), buf(256, D), buf(256, D),
        buf(5, 128, D), buf(5, 256, FU), buf(5, 128, D), buf(5, 256, FU),
        buf(S, D, dtype=F32), buf(S, 1, D, dtype=F32), buf(S, 1, D, dtype=F32), buf(2, 1, D, dtype=F32),
        buf(ND, 1, D, dtype=F32), buf(S, 1, D, dtype=F32), buf(IMG, 2 * S, PAT), buf(IMG, S, D), buf(S, IMG * PAT),
        buf(5, 256, FU, dtype=F32),
        pltpu.SemaphoreType.DMA((N_SEM,)), pltpu.SemaphoreType.DMA((N_SEM,)), pltpu.SemaphoreType.DMA((N_LOC,)),
    ]
    return pl.pallas_call(
        kernel,
        out_shape=(
            jax.ShapeDtypeStruct((IMG, 2 * S, PAT), BF16),
            jax.ShapeDtypeStruct((IMG, S, D), BF16),
            jax.ShapeDtypeStruct((S, D), F32),
            jax.ShapeDtypeStruct((D, FU), BF16),
            jax.ShapeDtypeStruct((FU, D), BF16),
        ),
        in_specs=[any_space, any_space, any_space, any_space, vmem_space, any_space, any_space],
        out_specs=(any_space,) * 5,
        scratch_shapes=scratch,
        compiler_params=pltpu.CompilerParams(
            collective_id=0, has_side_effects=True, vmem_limit_bytes=63 * 2**20
        ),
        cost_estimate=pl.CostEstimate(flops=21_000_000_000, bytes_accessed=40_000_000, transcendentals=2_000_000),
    )(codes, scales, tokens, gout, par_t, w_in, w_out)


def results_kernel(left, bg, par_t, gp, gwi, gwo, gt_o, gp_o, gwi_o, gwo_o):
    for k in range(left.shape[0]):
        right = jnp.concatenate([bg[k], par_t[...]], axis=0)
        gt_o[k] = dot(left[k], right, 0, 0).astype(BF16)
    gp_o[...] = gp[...]
    gwi_o[0] = gwi[...]
    gwo_o[0] = gwo[...]


def results(left, bg, par_t, gp, gwi, gwo):
    n = 2

    def whole(*shape):
        return pl.BlockSpec(shape, lambda i: (0,) * len(shape))

    def parts(*shape):
        return pl.BlockSpec(shape, lambda i: (i,) + (0,) * (len(shape) - 1))

    def rows(*shape):
        return pl.BlockSpec(shape, lambda i: (0, i, 0))

    return pl.pallas_call(
        results_kernel,
        grid=(n,),
        out_shape=(
            jax.ShapeDtypeStruct((IMG, PAT, D), BF16),
            jax.ShapeDtypeStruct((S, D), F32),
            jax.ShapeDtypeStruct((1, D, FU), BF16),
            jax.ShapeDtypeStruct((1, FU, D), BF16),
        ),
        in_specs=[
            parts(IMG // n, 2 * S, PAT), parts(IMG // n, S, D), whole(S, D), whole(S, D),
            parts(D // n, FU), parts(FU // n, D),
        ],
        out_specs=(parts(IMG // n, PAT, D), whole(S, D), rows(1, D // n, FU), rows(1, FU // n, D)),
        compiler_params=pltpu.CompilerParams(vmem_limit_bytes=60 * 2**20),
    )(left, bg, par_t, gp, gwi, gwo)


def local(tokens, slot_params, grad_out, slot_codes, scale_exps, w_in, w_out):
    par_t = slot_params.T
    left, bg, gp, gwi, gwo = layer(slot_codes, scale_exps.transpose(2, 1, 0), tokens.reshape(-1, D), grad_out.reshape(-1, D), par_t, w_in, w_out)
    grad_tokens, grad_params, grad_w_in, grad_w_out = results(left, bg, par_t, gp, gwi, gwo)
    return (grad_tokens, grad_params.T, grad_w_in, grad_w_out)


def solution(mesh):
    in_specs = (
        P(("dp", "expert"), None, None),
        P(),
        P(("dp", "expert"), None, None),
        P("dp", "expert", None),
        P("dp", "expert", None),
        P("expert", None, "dp"),
        P("expert", "dp", None),
    )
    out_specs = (
        P(("dp", "expert"), None, None),
        P(),
        P("expert", None, "dp"),
        P("expert", "dp", None),
    )
    return jax.shard_map(local, mesh=mesh, in_specs=in_specs, out_specs=out_specs, check_vma=False)
```

```python
import jax
import jax.numpy as jnp
from jax import lax
from jax.experimental import pallas as pl
from jax.experimental.pallas import tpu as pltpu
from jax.sharding import PartitionSpec as P

F32 = jnp.float32
BF16 = jnp.bfloat16
MESH = pl.DeviceIdType.MESH
gelu_coef = 0.7978845608028654

D, FU = 1280, 640
IMG, PAT, S = 16, 128, 16
ROWS = 1024
ND, NE = 8, 16

N1, N2 = 64, 192
X1, D1, G2, D2 = (0, N1), (64, N1), (128, N2), (320, N2)
M1, M2, G1, X2 = (512, N1), (576, N2), (768, N1), (832, N2)
ME = 512
KEEP = 512
AWAY = 128

W_IN, W_OUT = 0, 1
IN_HOP, GR_HOP, OUT_RS, IG_RS = 2, 11, 18, 22
GWO, GWI = 26, 31
A2A_G, A2A_O, A2A_I = 36, 37, 38
GP_A, GP_B, GP_C = 39, 40, 41
N_SEM = 42
L_CODE, L_WIN, L_WOUT, L_TOK, L_GO, L_LEFT, L_BG, L_SC, L_GWO, L_GWI, L_GP = 0, 1, 2, 3, 7, 11, 12, 13, 15, 20, 25
N_LOC = 26


def dot(a, b, ca, cb):
    return lax.dot_general(a, b, (((ca,), (cb,)), ((), ())), preferred_element_type=F32)


def gelu_both(x):
    x2 = x * x
    t = jnp.tanh(gelu_coef * (x + 0.044715 * x * x2))
    h = 0.5 * (1.0 + t)
    return x * h, h + 0.5 * x * (1.0 - t * t) * (gelu_coef + (gelu_coef * 3.0 * 0.044715) * x2)


def unit(u, skip=0, n=None):
    return pl.ds(u[0] + skip, n or u[1] - skip)


def put(ref, rows, value):
    for j in range(D // 128):
        ref[j, rows, :] = value[:, j * 128 : (j + 1) * 128]


def every_16th(ref, start):
    return jnp.concatenate([ref[j, pl.ds(start, 16, stride=16), :].astype(BF16) for j in range(D // 128)], axis=1)


def kernel(
    codes, scales, tokens, gout, par_t, w_in, w_out,
    left_out, bg_out, gp_out, gwi_out, gwo_out,
    code_v, sc_v, tok, go, win, wout, rin, rgr, hid, slope, pg,
    comb, disp, fbuf, gbuf, sg_send, back_o, back_i,
    ps_o, ps_i, kp_o, kp_i, rs_o, rs_i, h2_o, h2_i, fin_o, fin_i,
    gwo_s, gwi_s, gwo_r, gwi_r, gp_acc, gp_s, gp_r1, gp_m, gp_r2, gp_f, left, bgi, lg_all, gwi_own,
    s_sem, r_sem, l_sem,
):
    d, e = lax.axis_index("dp"), lax.axis_index("expert")
    xl, z, core = d // 4, lax.rem(d, 4), lax.rem(e, 2)
    z_near = z + 1 - 2 * lax.rem(z, 2)
    z_far = 3 - z
    z_pair = z_near * (1 - core) + z_far * core
    z_group = z_far * (1 - core) + z_near * core
    dev_x = ((1 - xl) * 4 + z, e)
    dev_p = (xl * 4 + z_pair, e)
    dev_g = (xl * 4 + z_group, e)
    others_e = [(d, lax.rem(e + k, NE)) for k in range(1, NE)]
    others_d = [(lax.rem(d + k, ND), e) for k in range(1, ND)]
    y, xh = e // 4, lax.rem(e // 2, 2)
    d_x = (1 - xl) * 4 + z

    def expert(j, k, x_hi):
        return lax.rem(y + j, 4) * 4 + x_hi * 2 + lax.rem(core + k, 2)

    def eighth(a):
        return (a // 4) * 2 + lax.rem(a, 2)

    turns = [(j, k) for j in range(4) for k in range(2)]
    home = [(d, expert(j, k, xh)) for j, k in turns[1:]]
    away = [(d_x, expert(j, k, 1 - xh)) for j, k in turns]

    def remote(src, dst, i, dev):
        return pltpu.make_async_remote_copy(
            src_ref=src, dst_ref=dst, send_sem=s_sem.at[i], recv_sem=r_sem.at[i], device_id=dev, device_id_type=MESH
        )

    def here(src, dst, i):
        return pltpu.make_async_copy(src, dst, l_sem.at[i])

    cp_code = here(codes.at[:, 0], code_v, L_CODE)
    cp_win = here(w_in.at[0], win.at[0], L_WIN)
    cp_wout = here(w_out.at[0], wout.at[0], L_WOUT)
    cp_sc = here(scales.at[:, 0], sc_v, L_SC)
    cp_code.start()
    cp_sc.start()

    def four(c):
        return pl.ds(pl.multiple_of(c * 4 * PAT, 4 * PAT), 4 * PAT)

    def image(i):
        return pl.ds(pl.multiple_of(i * PAT, PAT), PAT)

    def tok_copy(c):
        return here(tokens.at[four(c)], tok.at[four(c)], L_TOK + c)

    def go_copy(c):
        return here(gout.at[four(c)], go.at[four(c)], L_GO + c)

    barrier = pltpu.get_barrier_semaphore()
    for dev in others_e + others_d + away:
        pl.semaphore_signal(barrier, inc=1, device_id=dev, device_id_type=MESH)
    pl.semaphore_wait(barrier, NE + ND - 2 + 8)

    c_win = remote(w_in.at[0], win.at[1], W_IN, dev_p)
    c_wout = remote(w_out.at[0], wout.at[1], W_OUT, dev_p)
    c_win.start()

    def second_hops(buf, base, to):
        return [
            remote(buf.at[unit(X1)], buf.at[unit(D1)], base, dev_g),
            remote(buf.at[unit(X2, 0, 64)], buf.at[unit(D2, 0, 64)], base + 1, dev_g),
            remote(buf.at[unit(to[0], 64)], buf.at[unit(to[1], 64)], base + 2, dev_x),
        ]

    def in_hops(buf, base):
        first = [
            remote(buf.at[unit(M1)], buf.at[unit(X1)], base, dev_x),
            remote(buf.at[unit(X2, 64)], buf.at[unit(D2, 64)], base + 1, dev_g),
            remote(buf.at[unit(M2, 0, 64)], buf.at[unit(X2, 0, 64)], base + 2, dev_x),
            remote(buf.at[unit(M1)], buf.at[unit(G1)], base + 3, dev_g),
            remote(buf.at[unit(X2, 64)], buf.at[unit(M2, 64)], base + 4, dev_x),
            remote(buf.at[unit(M2, 0, 64)], buf.at[unit(G2, 0, 64)], base + 5, dev_g),
        ]
        return first, second_hops(buf, base + 6, (D2, G2))

    def row_hops(buf, base):
        first = [
            remote(buf.at[unit(M1)], buf.at[unit(X1)], base, dev_x),
            remote(buf.at[unit(M2)], buf.at[unit(G2)], base + 1, dev_g),
            remote(buf.at[unit(M2)], buf.at[unit(X2)], base + 2, dev_x),
            remote(buf.at[unit(M1)], buf.at[unit(G1)], base + 3, dev_g),
        ]
        return first, second_hops(buf, base + 4, (G2, D2))

    cp_code.wait()
    cp_sc.wait()

    sc = sc_v[...]
    fbuf[0, :, : D // 128] = jnp.where(sc == -9, 2.0**-18, jnp.where(sc == -8, 2.0**-17, 2.0**-16)).astype(F32).T

    def decode(t, carry):
        r = pl.ds(pl.multiple_of(t * 32, 32), 32)
        off = lax.rem(t, 2) - xh
        first = ME + off * off * (X2[0] + AWAY - N1 - ME)
        to = pl.ds(pl.multiple_of(first + (t // 2) * 32, 32), 32)
        scale = fbuf[0, r, : D // 128]
        for j in range(D // 128):
            code = code_v[r, j * 128 : (j + 1) * 128]
            exp = (code >> 3) & 15
            man = code & 7
            mag = jnp.where(exp == 0, man, (man + 8) << jnp.maximum(exp - 1, 0))
            val = jnp.where(code >= 128, -mag, mag).astype(F32) * scale[:, j : j + 1]
            rin[to, j * 128 : (j + 1) * 128] = val.astype(BF16)
        return carry

    lax.fori_loop(0, 8, decode, 0)
    in_1, in_2 = in_hops(rin, IN_HOP)
    for c in in_1:
        c.start()
    for c in range(4):
        tok_copy(c).start()
        go_copy(c).start()
    cp_win.start()
    cp_wout.start()

    def head(c, carry):
        tok_copy(c).wait()
        go_copy(c).wait()
        for k in range(4):
            i = c * 4 + k
            logits = dot(par_t[...], tok[image(i), :], 1, 1)
            e_m = jnp.exp(logits - jnp.max(logits, axis=1, keepdims=True))
            disp[i] = e_m / jnp.sum(e_m, axis=1, keepdims=True)
            e_s = jnp.exp(logits - jnp.max(logits, axis=0, keepdims=True))
            comb_i = e_s / jnp.sum(e_s, axis=0, keepdims=True)
            comb[i] = comb_i
            put(fbuf, pl.ds(pl.multiple_of(i * S, S), S), dot(comb_i.astype(BF16), go[image(i), :], 1, 0))
        return carry

    lax.fori_loop(0, 4, head, 0)
    for s in range(S):
        sg_send[s] = every_16th(fbuf, s)
    mine_16 = pl.ds(pl.multiple_of(e * IMG, IMG), IMG)
    at_home = pl.ds(pl.multiple_of(ME + eighth(e) * IMG, IMG), IMG)
    at_away = pl.ds(pl.multiple_of(ME + AWAY + eighth(e) * IMG, IMG), IMG)
    for dev in home:
        remote(sg_send.at[dev[1]], rgr.at[at_home], A2A_G, dev).start()
    for dev in away:
        remote(sg_send.at[dev[1]], rgr.at[at_away], A2A_G, dev).start()
    rgr[at_home, :] = sg_send[e]

    def wait_15(buf, i):
        both = remote(buf.at[pl.ds(0, 15 * IMG)], buf.at[pl.ds(0, 15 * IMG)], i, dev_x)
        both.wait()

    for c in in_1:
        c.wait_recv()
    for c in in_2:
        c.start()

    def pre(k, lo):
        a, sl = gelu_both(dot(rin[pl.ds(lo, 512), :], win[k], 1, 0))
        hid[k, pl.ds(lo, 512), :] = a.astype(BF16)
        slope[k, pl.ds(lo, 512), :] = sl.astype(BF16)

    cp_win.wait()
    cp_wout.wait()
    pre(0, 512)
    wait_15(rgr, A2A_G)
    gr_1, gr_2 = row_hops(rgr, GR_HOP)
    for c in gr_1:
        c.start()
    c_win.wait()
    c_wout.start()
    for c in in_2:
        c.wait_recv()
    pre(0, 0)
    pre(1, 512)
    for c in gr_1:
        c.wait_recv()
    for c in gr_2:
        c.start()
    pre(1, 0)

    def pre_grad(k, lo):
        hg = dot(rgr[pl.ds(lo, 512), :], wout[k], 1, 1)
        pg[k, pl.ds(lo, 512), :] = (hg * slope[k, pl.ds(lo, 512), :].astype(F32)).astype(BF16)

    pre_grad(0, 512)
    for c in gr_2:
        c.wait_recv()
    pre_grad(0, 0)

    def gwo_dot(k, c):
        return dot(hid[k, :, pl.ds(pl.multiple_of(c * 128, 128), 128)], rgr[...], 0, 0)

    def gwi_dot(k, c):
        return dot(rin[:, pl.ds(pl.multiple_of(c * 256, 256), 256)], pg[k], 0, 0)

    def gwo_copy(c):
        return remote(gwo_s.at[c], gwo_r.at[c], GWO + c, dev_p)

    def gwi_copy(c):
        return remote(gwi_s.at[c], gwi_r.at[c], GWI + c, dev_p)

    def fill_gwo(c, carry):
        gwo_s[c] = gwo_dot(1, c).astype(BF16)
        return carry

    lax.fori_loop(0, 5, fill_gwo, 0)

    def part(act, w, cw, r):
        return dot(act[0, r, :], w[0], 1, cw) + dot(act[1, r, :], w[1], 1, cw)

    def rs_hops(ps, rs, h2, base):
        first = [
            remote(ps.at[pl.ds(0, 2 * N1)], rs.at[pl.ds(0, 2 * N1)], base, dev_x),
            remote(ps.at[pl.ds(2 * N1, 2 * N2)], rs.at[pl.ds(2 * N1, 2 * N2)], base + 1, dev_g),
        ]
        second = [
            remote(h2.at[pl.ds(0, N1)], rs.at[pl.ds(512, N1)], base + 2, dev_g),
            remote(h2.at[pl.ds(N1, N2)], rs.at[pl.ds(512 + N1, N2)], base + 3, dev_x),
        ]
        return first, second

    def send_parts(act, w, cw, ps, first):
        for t in (1, 0):
            r = (pl.ds(0, 2 * N1), pl.ds(2 * N1, 2 * N2))[t]
            ps[r, :] = part(act, w, cw, r).astype(BF16)
            first[t].start()

    def keep_parts(act, w, cw, kp):
        for t in range(2):
            kp[pl.ds(t * 256, 256), :] = part(act, w, cw, pl.ds(KEEP + t * 256, 256))

    c_wout.wait()
    gwo_copy(0).start()
    out_1, out_2 = rs_hops(ps_o, rs_o, h2_o, OUT_RS)
    ig_1, ig_2 = rs_hops(ps_i, rs_i, h2_i, IG_RS)
    send_parts(hid, wout, 0, ps_o, out_1)
    pre_grad(1, 0)
    send_parts(pg, win, 1, ps_i, ig_1)
    keep_parts(hid, wout, 0, kp_o)
    pre_grad(1, 512)
    keep_parts(pg, win, 1, kp_i)

    def second_hop(first, second, kp, rs, h2):
        first[1].wait_recv()
        got = rs[pl.ds(2 * N1 + N2, N2), :].astype(F32)
        h2[pl.ds(N1, N2), :] = (kp[pl.ds(256 + N1, N2), :] + got).astype(BF16)
        second[1].start()
        first[0].wait_recv()
        got = rs[pl.ds(N1, N1), :].astype(F32)
        h2[pl.ds(0, N1), :] = (kp[pl.ds(256, N1), :] + got).astype(BF16)
        second[0].start()

    def finish_rows(second, kp, rs, fin, back, i):
        second[0].wait_recv()
        a, b, c = pl.ds(0, N1), pl.ds(0, N1), pl.ds(512, N1)
        fin[a, :] = (kp[a, :] + rs[b, :].astype(F32) + rs[c, :].astype(F32)).astype(BF16)
        second[1].wait_recv()
        a, b, c = pl.ds(N1, N2), pl.ds(2 * N1, N2), pl.ds(512 + N1, N2)
        fin[a, :] = (kp[a, :] + rs[b, :].astype(F32) + rs[c, :].astype(F32)).astype(BF16)
        for dev in home:
            src = pl.ds(pl.multiple_of(eighth(dev[1]) * IMG, IMG), IMG)
            remote(fin.at[src], back.at[mine_16], i, dev).start()
        for dev in away:
            src = pl.ds(pl.multiple_of(AWAY + eighth(dev[1]) * IMG, IMG), IMG)
            remote(fin.at[src], back.at[mine_16], i, dev).start()
        back[mine_16, :] = fin[pl.ds(pl.multiple_of(eighth(e) * IMG, IMG), IMG), :]

    second_hop(out_1, out_2, kp_o, rs_o, h2_o)
    gwo_copy(1).start()

    def fill_gwi(c, carry):
        gwi_s[c] = gwi_dot(1, c).astype(BF16)
        return carry

    lax.fori_loop(0, 5, fill_gwi, 0)
    second_hop(ig_1, ig_2, kp_i, rs_i, h2_i)
    for c in range(2, 5):
        gwo_copy(c).start()
    for c in range(5):
        gwi_copy(c).start()
    finish_rows(out_2, kp_o, rs_o, fin_o, back_o, A2A_O)

    def fill_own(c, carry):
        gwi_own[c] = gwi_dot(0, c)
        return carry

    lax.fori_loop(0, 5, fill_own, 0)
    finish_rows(ig_2, kp_i, rs_i, fin_i, back_i, A2A_I)

    def finish_gwo(c, carry):
        own = gwo_dot(0, c)
        gwo_copy(c).wait()
        gwo_r[c] = (own + gwo_r[c].astype(F32)).astype(BF16)
        here(gwo_r.at[c], gwo_out.at[pl.ds(pl.multiple_of(c * 128, 128), 128)], L_GWO + c).start()
        return carry

    def finish_gwi(c, carry):
        gwi_copy(c).wait()
        gwi_r[c] = (gwi_own[c] + gwi_r[c].astype(F32)).astype(BF16)
        here(gwi_r.at[c], gwi_out.at[pl.ds(pl.multiple_of(c * 256, 256), 256)], L_GWI + c).start()
        return carry

    wait_15(back_o, A2A_O)
    put(fbuf, slice(None), back_o[...].astype(F32))

    def tail_comb(c, carry):
        for k in range(4):
            i = c * 4 + k
            cg = dot(every_16th(fbuf, i), go[image(i), :], 1, 1)
            cm = comb[i]
            comb[i] = cm * (cg - jnp.sum(cm * cg, axis=0, keepdims=True))
        return carry

    lax.fori_loop(0, 4, tail_comb, 0)
    wait_15(back_i, A2A_I)
    put(gbuf, slice(None), back_i[...].astype(F32))

    cp_left = here(left, left_out, L_LEFT)
    cp_bg = here(bgi, bg_out, L_BG)

    def tail(c, carry):
        for k in range(4):
            i = c * 4 + k
            bg = every_16th(gbuf, i)
            dg = dot(bg, tok[image(i), :], 1, 1)
            dp = disp[i]
            lg = (comb[i] + dp * (dg - jnp.sum(dp * dg, axis=1, keepdims=True))).astype(BF16)
            lg_all[:, image(i)] = lg
            left[i, :S] = dp.astype(BF16)
            left[i, S:] = lg
            bgi[i] = bg
        return carry

    lax.fori_loop(0, 4, tail, 0)
    cp_left.start()
    cp_bg.start()

    gp = dot(lg_all[...], tok[...], 1, 0)
    for s in range(S):
        gp_s[s] = gp[s : s + 1, :]
    for dev in others_e:
        remote(gp_s.at[dev[1]], gp_r1.at[e], GP_A, dev).start()
    gp_r1[e] = gp_s[e]

    lax.fori_loop(0, 5, finish_gwo, 0)
    wait_many = remote(gp_s.at[pl.ds(0, NE - 1)], gp_r1.at[pl.ds(0, NE - 1)], GP_A, dev_x)
    wait_many.wait()
    total = gp_r1[0]
    for k in range(1, NE):
        total = total + gp_r1[k]
    gp_m[0] = total
    gp_r2[d] = total
    for dev in others_d:
        remote(gp_m.at[0], gp_r2.at[d], GP_B, dev).start()
    lax.fori_loop(0, 2, finish_gwi, 0)
    wait_many = remote(gp_r2.at[pl.ds(0, ND - 1)], gp_r2.at[pl.ds(0, ND - 1)], GP_B, dev_x)
    wait_many.wait()
    total = gp_r2[0]
    for k in range(1, ND):
        total = total + gp_r2[k]
    gp_m[1] = total
    gp_f[e] = total
    for dev in others_e:
        remote(gp_m.at[1], gp_f.at[e], GP_C, dev).start()

    lax.fori_loop(2, 5, finish_gwi, 0)
    wait_many = remote(gp_f.at[pl.ds(0, NE - 1)], gp_f.at[pl.ds(0, NE - 1)], GP_C, dev_x)
    wait_many.wait()
    for s in range(S):
        gp_acc[s : s + 1, :] = gp_f[s]
    cp_gp = here(gp_acc, gp_out, L_GP)
    cp_gp.start()

    for c in in_1 + in_2 + gr_1 + gr_2 + out_1 + out_2 + ig_1 + ig_2:
        c.wait_send()
    cp_left.wait()
    cp_bg.wait()
    for c in range(5):
        here(gwo_r.at[c], gwo_out.at[pl.ds(c * 128, 128)], L_GWO + c).wait()
        here(gwi_r.at[c], gwi_out.at[pl.ds(c * 256, 256)], L_GWI + c).wait()
    cp_gp.wait()


def layer(codes, scales, tokens, gout, par_t, w_in, w_out):
    any_space = pl.BlockSpec(memory_space=pl.ANY)
    vmem_space = pl.BlockSpec(memory_space=pltpu.VMEM)

    def buf(*shape, dtype=BF16):
        return pltpu.VMEM(shape, dtype)

    scratch = [
        buf(256, D, dtype=jnp.int32), buf(D // 128, 256, dtype=jnp.int32), buf(IMG * PAT, D), buf(IMG * PAT, D), buf(2, D, FU), buf(2, FU, D),
        buf(ROWS, D), buf(ROWS, D), buf(2, ROWS, FU), buf(2, ROWS, FU), buf(2, ROWS, FU),
        buf(IMG, S, PAT, dtype=F32), buf(IMG, S, PAT, dtype=F32), buf(D // 128, 256, 128, dtype=F32), buf(D // 128, 256, 128, dtype=F32),
        buf(S, IMG, D), buf(256, D), buf(256, D),
        buf(512, D), buf(512, D), buf(512, D, dtype=F32), buf(512, D, dtype=F32),
        buf(768, D), buf(768, D), buf(256, D), buf(256, D), buf(256, D), buf(256, D),
        buf(5, 128, D), buf(5, 256, FU), buf(5, 128, D), buf(5, 256, FU),
        buf(S, D, dtype=F32), buf(S, 1, D, dtype=F32), buf(S, 1, D, dtype=F32), buf(2, 1, D, dtype=F32),
        buf(ND, 1, D, dtype=F32), buf(S, 1, D, dtype=F32), buf(IMG, 2 * S, PAT), buf(IMG, S, D), buf(S, IMG * PAT),
        buf(5, 256, FU, dtype=F32),
        pltpu.SemaphoreType.DMA((N_SEM,)), pltpu.SemaphoreType.DMA((N_SEM,)), pltpu.SemaphoreType.DMA((N_LOC,)),
    ]
    return pl.pallas_call(
        kernel,
        out_shape=(
            jax.ShapeDtypeStruct((IMG, 2 * S, PAT), BF16),
            jax.ShapeDtypeStruct((IMG, S, D), BF16),
            jax.ShapeDtypeStruct((S, D), F32),
            jax.ShapeDtypeStruct((D, FU), BF16),
            jax.ShapeDtypeStruct((FU, D), BF16),
        ),
        in_specs=[any_space, any_space, any_space, any_space, vmem_space, any_space, any_space],
        out_specs=(any_space,) * 5,
        scratch_shapes=scratch,
        compiler_params=pltpu.CompilerParams(
            collective_id=0, has_side_effects=True, vmem_limit_bytes=63 * 2**20
        ),
        cost_estimate=pl.CostEstimate(flops=21_000_000_000, bytes_accessed=40_000_000, transcendentals=2_000_000),
    )(codes, scales, tokens, gout, par_t, w_in, w_out)


def results_kernel(left, bg, par_t, gp, gwi, gwo, gt_o, gp_o, gwi_o, gwo_o):
    for k in range(left.shape[0]):
        right = jnp.concatenate([bg[k], par_t[...]], axis=0)
        gt_o[k] = dot(left[k], right, 0, 0).astype(BF16)
    gp_o[...] = gp[...]
    gwi_o[0] = gwi[...]
    gwo_o[0] = gwo[...]


def results(left, bg, par_t, gp, gwi, gwo):
    n = 2

    def whole(*shape):
        return pl.BlockSpec(shape, lambda i: (0,) * len(shape))

    def parts(*shape):
        return pl.BlockSpec(shape, lambda i: (i,) + (0,) * (len(shape) - 1))

    def rows(*shape):
        return pl.BlockSpec(shape, lambda i: (0, i, 0))

    return pl.pallas_call(
        results_kernel,
        grid=(n,),
        out_shape=(
            jax.ShapeDtypeStruct((IMG, PAT, D), BF16),
            jax.ShapeDtypeStruct((S, D), F32),
            jax.ShapeDtypeStruct((1, D, FU), BF16),
            jax.ShapeDtypeStruct((1, FU, D), BF16),
        ),
        in_specs=[
            parts(IMG // n, 2 * S, PAT), parts(IMG // n, S, D), whole(S, D), whole(S, D),
            parts(D // n, FU), parts(FU // n, D),
        ],
        out_specs=(parts(IMG // n, PAT, D), whole(S, D), rows(1, D // n, FU), rows(1, FU // n, D)),
        compiler_params=pltpu.CompilerParams(vmem_limit_bytes=60 * 2**20),
    )(left, bg, par_t, gp, gwi, gwo)


def local(tokens, slot_params, grad_out, slot_codes, scale_exps, w_in, w_out):
    par_t = slot_params.T
    left, bg, gp, gwi, gwo = layer(slot_codes, scale_exps.transpose(2, 1, 0), tokens.reshape(-1, D), grad_out.reshape(-1, D), par_t, w_in, w_out)
    grad_tokens, grad_params, grad_w_in, grad_w_out = results(left, bg, par_t, gp, gwi, gwo)
    return (grad_tokens, grad_params.T, grad_w_in, grad_w_out)


def solution(mesh):
    in_specs = (
        P(("dp", "expert"), None, None),
        P(),
        P(("dp", "expert"), None, None),
        P("dp", "expert", None),
        P("dp", "expert", None),
        P("expert", None, "dp"),
        P("expert", "dp", None),
    )
    out_specs = (
        P(("dp", "expert"), None, None),
        P(),
        P("expert", None, "dp"),
        P("expert", "dp", None),
    )
    return jax.shard_map(local, mesh=mesh, in_specs=in_specs, out_specs=out_specs, check_vma=False)
```

```python
import jax
import jax.numpy as jnp
from jax import lax
from jax.experimental import pallas as pl
from jax.experimental.pallas import tpu as pltpu
from jax.sharding import PartitionSpec as P

F32 = jnp.float32
BF16 = jnp.bfloat16
MESH = pl.DeviceIdType.MESH
gelu_coef = 0.7978845608028654

D, FU = 1280, 640
IMG, PAT, S = 16, 128, 16
ROWS = 1024
ND, NE = 8, 16

N1, N2 = 64, 192
X1, D1, G2, D2 = (0, N1), (64, N1), (128, N2), (320, N2)
M1, M2, G1, X2 = (512, N1), (576, N2), (768, N1), (832, N2)
ME = 512
KEEP = 512
AWAY = 128

W_IN, W_OUT = 0, 1
IN_HOP, GR_HOP, OUT_RS, IG_RS = 2, 11, 18, 22
GWO, GWI = 26, 31
A2A_G, A2A_O, A2A_I = 36, 37, 38
GP_A, GP_B, GP_C = 39, 40, 41
N_SEM = 42
L_CODE, L_WIN, L_WOUT, L_TOK, L_GO, L_LEFT, L_BG, L_SC, L_GWO, L_GWI, L_GP = 0, 1, 2, 3, 7, 11, 12, 13, 15, 20, 25
N_LOC = 26


def dot(a, b, ca, cb):
    return lax.dot_general(a, b, (((ca,), (cb,)), ((), ())), preferred_element_type=F32)


def gelu_both(x):
    x2 = x * x
    t = jnp.tanh(gelu_coef * (x + 0.044715 * x * x2))
    h = 0.5 * (1.0 + t)
    return x * h, h + 0.5 * x * (1.0 - t * t) * (gelu_coef + (gelu_coef * 3.0 * 0.044715) * x2)


def unit(u, skip=0, n=None):
    return pl.ds(u[0] + skip, n or u[1] - skip)


def put(ref, rows, value):
    for j in range(D // 128):
        ref[j, rows, :] = value[:, j * 128 : (j + 1) * 128]


def every_16th(ref, start):
    return jnp.concatenate([ref[j, pl.ds(start, 16, stride=16), :].astype(BF16) for j in range(D // 128)], axis=1)


def kernel(
    codes, scales, tokens, gout, par_t, w_in, w_out,
    left_out, bg_out, gp_out, gwi_out, gwo_out,
    code_v, sc_v, tok, go, win, wout, rin, rgr, hid, slope, pg,
    comb, disp, fbuf, gbuf, sg_send, back_o, back_i,
    ps_o, ps_i, kp_o, kp_i, rs_o, rs_i, h2_o, h2_i, fin_o, fin_i,
    gwo_s, gwi_s, gwo_r, gwi_r, gp_acc, gp_s, gp_r1, gp_m, gp_r2, gp_f, left, bgi, lg_all, gwi_own,
    s_sem, r_sem, l_sem,
):
    d, e = lax.axis_index("dp"), lax.axis_index("expert")
    xl, z, core = d // 4, lax.rem(d, 4), lax.rem(e, 2)
    z_near = z + 1 - 2 * lax.rem(z, 2)
    z_far = 3 - z
    z_pair = z_near * (1 - core) + z_far * core
    z_group = z_far * (1 - core) + z_near * core
    dev_x = ((1 - xl) * 4 + z, e)
    dev_p = (xl * 4 + z_pair, e)
    dev_g = (xl * 4 + z_group, e)
    others_e = [(d, lax.rem(e + k, NE)) for k in range(1, NE)]
    others_d = [(lax.rem(d + k, ND), e) for k in range(1, ND)]
    y, xh = e // 4, lax.rem(e // 2, 2)
    d_x = (1 - xl) * 4 + z

    def expert(j, k, x_hi):
        return lax.rem(y + j, 4) * 4 + x_hi * 2 + lax.rem(core + k, 2)

    def eighth(a):
        return (a // 4) * 2 + lax.rem(a, 2)

    turns = [(j, k) for j in range(4) for k in range(2)]
    home = [(d, expert(j, k, xh)) for j, k in turns[1:]]
    away = [(d_x, expert(j, k, 1 - xh)) for j, k in turns]

    def remote(src, dst, i, dev):
        return pltpu.make_async_remote_copy(
            src_ref=src, dst_ref=dst, send_sem=s_sem.at[i], recv_sem=r_sem.at[i], device_id=dev, device_id_type=MESH
        )

    def here(src, dst, i):
        return pltpu.make_async_copy(src, dst, l_sem.at[i])

    cp_code = here(codes.at[:, 0], code_v, L_CODE)
    cp_win = here(w_in.at[0], win.at[0], L_WIN)
    cp_wout = here(w_out.at[0], wout.at[0], L_WOUT)
    cp_sc = here(scales.at[:, 0], sc_v, L_SC)
    cp_code.start()
    cp_sc.start()

    def four(c):
        return pl.ds(pl.multiple_of(c * 4 * PAT, 4 * PAT), 4 * PAT)

    def image(i):
        return pl.ds(pl.multiple_of(i * PAT, PAT), PAT)

    def tok_copy(c):
        return here(tokens.at[four(c)], tok.at[four(c)], L_TOK + c)

    def go_copy(c):
        return here(gout.at[four(c)], go.at[four(c)], L_GO + c)

    barrier = pltpu.get_barrier_semaphore()
    for dev in others_e + others_d + away:
        pl.semaphore_signal(barrier, inc=1, device_id=dev, device_id_type=MESH)
    pl.semaphore_wait(barrier, NE + ND - 2 + 8)

    c_win = remote(w_in.at[0], win.at[1], W_IN, dev_p)
    c_wout = remote(w_out.at[0], wout.at[1], W_OUT, dev_p)
    c_win.start()

    def second_hops(buf, base, to):
        return [
            remote(buf.at[unit(X1)], buf.at[unit(D1)], base, dev_g),
            remote(buf.at[unit(X2, 0, 64)], buf.at[unit(D2, 0, 64)], base + 1, dev_g),
            remote(buf.at[unit(to[0], 64)], buf.at[unit(to[1], 64)], base + 2, dev_x),
        ]

    def in_hops(buf, base):
        first = [
            remote(buf.at[unit(M1)], buf.at[unit(X1)], base, dev_x),
            remote(buf.at[unit(X2, 64)], buf.at[unit(D2, 64)], base + 1, dev_g),
            remote(buf.at[unit(M2, 0, 64)], buf.at[unit(X2, 0, 64)], base + 2, dev_x),
            remote(buf.at[unit(M1)], buf.at[unit(G1)], base + 3, dev_g),
            remote(buf.at[unit(X2, 64)], buf.at[unit(M2, 64)], base + 4, dev_x),
            remote(buf.at[unit(M2, 0, 64)], buf.at[unit(G2, 0, 64)], base + 5, dev_g),
        ]
        return first, second_hops(buf, base + 6, (D2, G2))

    def row_hops(buf, base):
        first = [
            remote(buf.at[unit(M1)], buf.at[unit(X1)], base, dev_x),
            remote(buf.at[unit(M2)], buf.at[unit(G2)], base + 1, dev_g),
            remote(buf.at[unit(M2)], buf.at[unit(X2)], base + 2, dev_x),
            remote(buf.at[unit(M1)], buf.at[unit(G1)], base + 3, dev_g),
        ]
        return first, second_hops(buf, base + 4, (G2, D2))

    cp_code.wait()
    cp_sc.wait()

    sc = sc_v[...]
    fbuf[0, :, : D // 128] = jnp.where(sc == -9, 2.0**-18, jnp.where(sc == -8, 2.0**-17, 2.0**-16)).astype(F32).T

    def decode(t, carry):
        r = pl.ds(pl.multiple_of(t * 32, 32), 32)
        off = lax.rem(t, 2) - xh
        first = ME + off * off * (X2[0] + AWAY - N1 - ME)
        to = pl.ds(pl.multiple_of(first + (t // 2) * 32, 32), 32)
        scale = fbuf[0, r, : D // 128]
        for j in range(D // 128):
            code = code_v[r, j * 128 : (j + 1) * 128]
            exp = (code >> 3) & 15
            man = code & 7
            mag = jnp.where(exp == 0, man, (man + 8) << jnp.maximum(exp - 1, 0))
            val = jnp.where(code >= 128, -mag, mag).astype(F32) * scale[:, j : j + 1]
            rin[to, j * 128 : (j + 1) * 128] = val.astype(BF16)
        return carry

    lax.fori_loop(0, 8, decode, 0)
    in_1, in_2 = in_hops(rin, IN_HOP)
    for c in in_1:
        c.start()
    for c in range(4):
        tok_copy(c).start()
        go_copy(c).start()
    cp_win.start()
    cp_wout.start()

    def head(c, carry):
        tok_copy(c).wait()
        go_copy(c).wait()
        for k in range(4):
            i = c * 4 + k
            logits = dot(par_t[...], tok[image(i), :], 1, 1)
            e_m = jnp.exp(logits - jnp.max(logits, axis=1, keepdims=True))
            disp[i] = e_m / jnp.sum(e_m, axis=1, keepdims=True)
            e_s = jnp.exp(logits - jnp.max(logits, axis=0, keepdims=True))
            comb_i = e_s / jnp.sum(e_s, axis=0, keepdims=True)
            comb[i] = comb_i
            put(fbuf, pl.ds(pl.multiple_of(i * S, S), S), dot(comb_i.astype(BF16), go[image(i), :], 1, 0))
        return carry

    lax.fori_loop(0, 4, head, 0)
    for s in range(S):
        sg_send[s] = every_16th(fbuf, s)
    mine_16 = pl.ds(pl.multiple_of(e * IMG, IMG), IMG)
    at_home = pl.ds(pl.multiple_of(ME + eighth(e) * IMG, IMG), IMG)
    at_away = pl.ds(pl.multiple_of(ME + AWAY + eighth(e) * IMG, IMG), IMG)
    for dev in home:
        remote(sg_send.at[dev[1]], rgr.at[at_home], A2A_G, dev).start()
    for dev in away:
        remote(sg_send.at[dev[1]], rgr.at[at_away], A2A_G, dev).start()
    rgr[at_home, :] = sg_send[e]

    def wait_15(buf, i):
        both = remote(buf.at[pl.ds(0, 15 * IMG)], buf.at[pl.ds(0, 15 * IMG)], i, dev_x)
        both.wait()

    for c in in_1:
        c.wait_recv()
    for c in in_2:
        c.start()

    def pre(k, lo):
        a, sl = gelu_both(dot(rin[pl.ds(lo, 512), :], win[k], 1, 0))
        hid[k, pl.ds(lo, 512), :] = a.astype(BF16)
        slope[k, pl.ds(lo, 512), :] = sl.astype(BF16)

    cp_win.wait()
    cp_wout.wait()
    wait_15(rgr, A2A_G)
    gr_1, gr_2 = row_hops(rgr, GR_HOP)
    for c in gr_1:
        c.start()
    pre(0, 512)
    c_wout.start()
    c_win.wait()
    for c in in_2:
        c.wait_recv()
    pre(0, 0)
    pre(1, 512)
    for c in gr_1:
        c.wait_recv()
    for c in gr_2:
        c.start()
    pre(1, 0)

    def pre_grad(k, lo):
        hg = dot(rgr[pl.ds(lo, 512), :], wout[k], 1, 1)
        pg[k, pl.ds(lo, 512), :] = (hg * slope[k, pl.ds(lo, 512), :].astype(F32)).astype(BF16)

    pre_grad(0, 512)
    for c in gr_2:
        c.wait_recv()
    pre_grad(0, 0)

    def gwo_dot(k, c):
        return dot(hid[k, :, pl.ds(pl.multiple_of(c * 128, 128), 128)], rgr[...], 0, 0)

    def gwi_dot(k, c):
        return dot(rin[:, pl.ds(pl.multiple_of(c * 256, 256), 256)], pg[k], 0, 0)

    def gwo_copy(c):
        return remote(gwo_s.at[c], gwo_r.at[c], GWO + c, dev_p)

    def gwi_copy(c):
        return remote(gwi_s.at[c], gwi_r.at[c], GWI + c, dev_p)

    def fill_gwo(c, carry):
        gwo_s[c] = gwo_dot(1, c).astype(BF16)
        return carry

    lax.fori_loop(0, 5, fill_gwo, 0)

    def part(act, w, cw, r):
        return dot(act[0, r, :], w[0], 1, cw) + dot(act[1, r, :], w[1], 1, cw)

    def rs_hops(ps, rs, h2, base):
        first = [
            remote(ps.at[pl.ds(0, 2 * N1)], rs.at[pl.ds(0, 2 * N1)], base, dev_x),
            remote(ps.at[pl.ds(2 * N1, 2 * N2)], rs.at[pl.ds(2 * N1, 2 * N2)], base + 1, dev_g),
        ]
        second = [
            remote(h2.at[pl.ds(0, N1)], rs.at[pl.ds(512, N1)], base + 2, dev_g),
            remote(h2.at[pl.ds(N1, N2)], rs.at[pl.ds(512 + N1, N2)], base + 3, dev_x),
        ]
        return first, second

    def send_parts(act, w, cw, ps, first):
        for t in (1, 0):
            r = (pl.ds(0, 2 * N1), pl.ds(2 * N1, 2 * N2))[t]
            ps[r, :] = part(act, w, cw, r).astype(BF16)
            first[t].start()

    def keep_parts(act, w, cw, kp):
        for t in range(2):
            kp[pl.ds(t * 256, 256), :] = part(act, w, cw, pl.ds(KEEP + t * 256, 256))

    gwo_copy(0).start()
    c_wout.wait()
    out_1, out_2 = rs_hops(ps_o, rs_o, h2_o, OUT_RS)
    ig_1, ig_2 = rs_hops(ps_i, rs_i, h2_i, IG_RS)
    send_parts(hid, wout, 0, ps_o, out_1)
    pre_grad(1, 0)
    send_parts(pg, win, 1, ps_i, ig_1)
    keep_parts(hid, wout, 0, kp_o)
    pre_grad(1, 512)
    keep_parts(pg, win, 1, kp_i)

    def second_hop(first, second, kp, rs, h2):
        first[1].wait_recv()
        got = rs[pl.ds(2 * N1 + N2, N2), :].astype(F32)
        h2[pl.ds(N1, N2), :] = (kp[pl.ds(256 + N1, N2), :] + got).astype(BF16)
        second[1].start()
        first[0].wait_recv()
        got = rs[pl.ds(N1, N1), :].astype(F32)
        h2[pl.ds(0, N1), :] = (kp[pl.ds(256, N1), :] + got).astype(BF16)
        second[0].start()

    def finish_rows(second, kp, rs, fin, back, i):
        second[0].wait_recv()
        a, b, c = pl.ds(0, N1), pl.ds(0, N1), pl.ds(512, N1)
        fin[a, :] = (kp[a, :] + rs[b, :].astype(F32) + rs[c, :].astype(F32)).astype(BF16)
        second[1].wait_recv()
        a, b, c = pl.ds(N1, N2), pl.ds(2 * N1, N2), pl.ds(512 + N1, N2)
        fin[a, :] = (kp[a, :] + rs[b, :].astype(F32) + rs[c, :].astype(F32)).astype(BF16)
        for dev in home:
            src = pl.ds(pl.multiple_of(eighth(dev[1]) * IMG, IMG), IMG)
            remote(fin.at[src], back.at[mine_16], i, dev).start()
        for dev in away:
            src = pl.ds(pl.multiple_of(AWAY + eighth(dev[1]) * IMG, IMG), IMG)
            remote(fin.at[src], back.at[mine_16], i, dev).start()
        back[mine_16, :] = fin[pl.ds(pl.multiple_of(eighth(e) * IMG, IMG), IMG), :]

    second_hop(out_1, out_2, kp_o, rs_o, h2_o)

    def fill_gwi(c, carry):
        gwi_s[c] = gwi_dot(1, c).astype(BF16)
        return carry

    lax.fori_loop(0, 5, fill_gwi, 0)
    second_hop(ig_1, ig_2, kp_i, rs_i, h2_i)
    for c in range(1, 5):
        gwo_copy(c).start()
    for c in range(5):
        gwi_copy(c).start()
    finish_rows(out_2, kp_o, rs_o, fin_o, back_o, A2A_O)

    def fill_own(c, carry):
        gwi_own[c] = gwi_dot(0, c)
        return carry

    lax.fori_loop(0, 5, fill_own, 0)
    finish_rows(ig_2, kp_i, rs_i, fin_i, back_i, A2A_I)

    def finish_gwo(c, carry):
        own = gwo_dot(0, c)
        gwo_copy(c).wait()
        gwo_r[c] = (own + gwo_r[c].astype(F32)).astype(BF16)
        here(gwo_r.at[c], gwo_out.at[pl.ds(pl.multiple_of(c * 128, 128), 128)], L_GWO + c).start()
        return carry

    def finish_gwi(c, carry):
        gwi_copy(c).wait()
        gwi_r[c] = (gwi_own[c] + gwi_r[c].astype(F32)).astype(BF16)
        here(gwi_r.at[c], gwi_out.at[pl.ds(pl.multiple_of(c * 256, 256), 256)], L_GWI + c).start()
        return carry

    wait_15(back_o, A2A_O)
    put(fbuf, slice(None), back_o[...].astype(F32))

    def tail_comb(c, carry):
        for k in range(8):
            i = c * 8 + k
            cg = dot(every_16th(fbuf, i), go[image(i), :], 1, 1)
            cm = comb[i]
            comb[i] = cm * (cg - jnp.sum(cm * cg, axis=0, keepdims=True))
        return carry

    lax.fori_loop(0, 2, tail_comb, 0)
    wait_15(back_i, A2A_I)
    put(gbuf, slice(None), back_i[...].astype(F32))

    cp_left = here(left, left_out, L_LEFT)
    cp_bg = here(bgi, bg_out, L_BG)

    def tail(c, carry):
        for k in range(8):
            i = c * 8 + k
            bg = every_16th(gbuf, i)
            dg = dot(bg, tok[image(i), :], 1, 1)
            dp = disp[i]
            lg = (comb[i] + dp * (dg - jnp.sum(dp * dg, axis=1, keepdims=True))).astype(BF16)
            lg_all[:, image(i)] = lg
            left[i, :S] = dp.astype(BF16)
            left[i, S:] = lg
            bgi[i] = bg
        return carry

    lax.fori_loop(0, 2, tail, 0)
    cp_left.start()
    cp_bg.start()

    gp = dot(lg_all[...], tok[...], 1, 0)
    for s in range(S):
        gp_s[s] = gp[s : s + 1, :]
    for dev in others_e:
        remote(gp_s.at[dev[1]], gp_r1.at[e], GP_A, dev).start()
    gp_r1[e] = gp_s[e]

    wait_many = remote(gp_s.at[pl.ds(0, NE - 1)], gp_r1.at[pl.ds(0, NE - 1)], GP_A, dev_x)
    wait_many.wait()
    total = gp_r1[0]
    for k in range(1, NE):
        total = total + gp_r1[k]
    gp_m[0] = total
    gp_r2[d] = total
    for dev in others_d:
        remote(gp_m.at[0], gp_r2.at[d], GP_B, dev).start()
    wait_many = remote(gp_r2.at[pl.ds(0, ND - 1)], gp_r2.at[pl.ds(0, ND - 1)], GP_B, dev_x)
    wait_many.wait()
    total = gp_r2[0]
    for k in range(1, ND):
        total = total + gp_r2[k]
    gp_m[1] = total
    gp_f[e] = total
    for dev in others_e:
        remote(gp_m.at[1], gp_f.at[e], GP_C, dev).start()

    lax.fori_loop(0, 5, finish_gwo, 0)
    lax.fori_loop(0, 5, finish_gwi, 0)
    wait_many = remote(gp_f.at[pl.ds(0, NE - 1)], gp_f.at[pl.ds(0, NE - 1)], GP_C, dev_x)
    wait_many.wait()
    for s in range(S):
        gp_acc[s : s + 1, :] = gp_f[s]
    cp_gp = here(gp_acc, gp_out, L_GP)
    cp_gp.start()

    for c in in_1 + in_2 + gr_1 + gr_2 + out_1 + out_2 + ig_1 + ig_2:
        c.wait_send()
    cp_left.wait()
    cp_bg.wait()
    for c in range(5):
        here(gwo_r.at[c], gwo_out.at[pl.ds(c * 128, 128)], L_GWO + c).wait()
        here(gwi_r.at[c], gwi_out.at[pl.ds(c * 256, 256)], L_GWI + c).wait()
    cp_gp.wait()


def layer(codes, scales, tokens, gout, par_t, w_in, w_out):
    any_space = pl.BlockSpec(memory_space=pl.ANY)
    vmem_space = pl.BlockSpec(memory_space=pltpu.VMEM)

    def buf(*shape, dtype=BF16):
        return pltpu.VMEM(shape, dtype)

    scratch = [
        buf(256, D, dtype=jnp.int32), buf(D // 128, 256, dtype=jnp.int32), buf(IMG * PAT, D), buf(IMG * PAT, D), buf(2, D, FU), buf(2, FU, D),
        buf(ROWS, D), buf(ROWS, D), buf(2, ROWS, FU), buf(2, ROWS, FU), buf(2, ROWS, FU),
        buf(IMG, S, PAT, dtype=F32), buf(IMG, S, PAT, dtype=F32), buf(D // 128, 256, 128, dtype=F32), buf(D // 128, 256, 128, dtype=F32),
        buf(S, IMG, D), buf(256, D), buf(256, D),
        buf(512, D), buf(512, D), buf(512, D, dtype=F32), buf(512, D, dtype=F32),
        buf(768, D), buf(768, D), buf(256, D), buf(256, D), buf(256, D), buf(256, D),
        buf(5, 128, D), buf(5, 256, FU), buf(5, 128, D), buf(5, 256, FU),
        buf(S, D, dtype=F32), buf(S, 1, D, dtype=F32), buf(S, 1, D, dtype=F32), buf(2, 1, D, dtype=F32),
        buf(ND, 1, D, dtype=F32), buf(S, 1, D, dtype=F32), buf(IMG, 2 * S, PAT), buf(IMG, S, D), buf(S, IMG * PAT),
        buf(5, 256, FU, dtype=F32),
        pltpu.SemaphoreType.DMA((N_SEM,)), pltpu.SemaphoreType.DMA((N_SEM,)), pltpu.SemaphoreType.DMA((N_LOC,)),
    ]
    return pl.pallas_call(
        kernel,
        out_shape=(
            jax.ShapeDtypeStruct((IMG, 2 * S, PAT), BF16),
            jax.ShapeDtypeStruct((IMG, S, D), BF16),
            jax.ShapeDtypeStruct((S, D), F32),
            jax.ShapeDtypeStruct((D, FU), BF16),
            jax.ShapeDtypeStruct((FU, D), BF16),
        ),
        in_specs=[any_space, any_space, any_space, any_space, vmem_space, any_space, any_space],
        out_specs=(any_space,) * 5,
        scratch_shapes=scratch,
        compiler_params=pltpu.CompilerParams(
            collective_id=0, has_side_effects=True, vmem_limit_bytes=63 * 2**20
        ),
        cost_estimate=pl.CostEstimate(flops=21_000_000_000, bytes_accessed=40_000_000, transcendentals=2_000_000),
    )(codes, scales, tokens, gout, par_t, w_in, w_out)


def results_kernel(left, bg, par_t, gp, gwi, gwo, gt_o, gp_o, gwi_o, gwo_o):
    for k in range(left.shape[0]):
        right = jnp.concatenate([bg[k], par_t[...]], axis=0)
        gt_o[k] = dot(left[k], right, 0, 0).astype(BF16)
    gp_o[...] = gp[...]
    gwi_o[0] = gwi[...]
    gwo_o[0] = gwo[...]


def results(left, bg, par_t, gp, gwi, gwo):
    n = 2

    def whole(*shape):
        return pl.BlockSpec(shape, lambda i: (0,) * len(shape))

    def parts(*shape):
        return pl.BlockSpec(shape, lambda i: (i,) + (0,) * (len(shape) - 1))

    def rows(*shape):
        return pl.BlockSpec(shape, lambda i: (0, i, 0))

    return pl.pallas_call(
        results_kernel,
        grid=(n,),
        out_shape=(
            jax.ShapeDtypeStruct((IMG, PAT, D), BF16),
            jax.ShapeDtypeStruct((S, D), F32),
            jax.ShapeDtypeStruct((1, D, FU), BF16),
            jax.ShapeDtypeStruct((1, FU, D), BF16),
        ),
        in_specs=[
            parts(IMG // n, 2 * S, PAT), parts(IMG // n, S, D), whole(S, D), whole(S, D),
            parts(D // n, FU), parts(FU // n, D),
        ],
        out_specs=(parts(IMG // n, PAT, D), whole(S, D), rows(1, D // n, FU), rows(1, FU // n, D)),
        compiler_params=pltpu.CompilerParams(vmem_limit_bytes=60 * 2**20),
    )(left, bg, par_t, gp, gwi, gwo)


def local(tokens, slot_params, grad_out, slot_codes, scale_exps, w_in, w_out):
    par_t = slot_params.T
    left, bg, gp, gwi, gwo = layer(slot_codes, scale_exps.transpose(2, 1, 0), tokens.reshape(-1, D), grad_out.reshape(-1, D), par_t, w_in, w_out)
    grad_tokens, grad_params, grad_w_in, grad_w_out = results(left, bg, par_t, gp, gwi, gwo)
    return (grad_tokens, grad_params.T, grad_w_in, grad_w_out)


def solution(mesh):
    in_specs = (
        P(("dp", "expert"), None, None),
        P(),
        P(("dp", "expert"), None, None),
        P("dp", "expert", None),
        P("dp", "expert", None),
        P("expert", None, "dp"),
        P("expert", "dp", None),
    )
    out_specs = (
        P(("dp", "expert"), None, None),
        P(),
        P("expert", None, "dp"),
        P("expert", "dp", None),
    )
    return jax.shard_map(local, mesh=mesh, in_specs=in_specs, out_specs=out_specs, check_vma=False)
```
